768 devices in a mesh: dp: 96 (over y, z), tensor: 8 (over x, core).
Axes of the slice: x: 4, y: 8, z: 12, core: 2. Of those that a mesh axis runs over, the one named last changes fastest.
Arguments:
- activations: bfloat16 [49152, 8192], P('dp', 'tensor'), may hold values from -6 to 6
- cotangent: bfloat16 [49152, 8192], P('dp', 'tensor'), may hold values from -0.0625 to 0.0625
- factor_down: float32 [8192, 64], P('tensor'), may hold values from -0.0625 to 0.0625
- factor_up: float32 [64, 8192], P(None, 'tensor'), may hold values from -0.75 to 0.75
- first_moment: float32 [8, 135168], P('tensor', 'dp'), may hold values from -4 to 4
- second_moment: float32 [8, 135168], P('tensor', 'dp'), may hold values from 0.01 to 1
- piece_lengths: int32 [8, 64], P('tensor'), may hold values from 1 to 4224, 135168 in all within a row
- writers: int32 [8, 64], P('tensor'), may hold values from 0 to 95
Outputs:
- partition: float32 [3, 8, 135168], P(None, 'tensor', 'dp')
- written: float32 [3, 96, 8, 135168], P(None, 'dp', 'tensor')
The draws below stay inside these ranges and needn't reach their ends.
Inputs may be any that keep to these rules, and one draw needn't show every extreme that they name: `piece_lengths`: each row sums to 135168.
All inputs are finite; a program needn't handle non-finite values.
Results may differ from the reference program's by a relative error of at most 0.017.
Values may be sent and summed in bfloat16 or wider, within the bound.
No kernel may reach another device: no remote copies, remote signals or barrier semaphores. Data moves between devices by JAX's collectives and lax.ppermute only.
A program may use at most 64 MiB of HBM per device.

```python
import math
import jax
import jax.numpy as jnp
import numpy as np
from jax import lax

D = 8192
R = 64
SEGS = 64
TOKENS = 49152
FLAT_PAD = 135168
N_DP = 96
N_TENSOR = 8


def with_ends(result, stream_key, least, high):
    longest = result.shape.index(max(result.shape))
    spots = []
    for shift in (0, 1):
        where = [jax.random.randint(jax.random.fold_in(stream_key, axis), (), 0, length) for axis, length in enumerate(result.shape)]
        where[longest] = (where[longest] + shift) % result.shape[longest]
        spots.append(tuple(where))
    return result.at[spots[0]].set(least).at[spots[1]].set(high)


def shard_levels(own_key, extent, cuts, low, top_value):
    factor_of = 1.0
    for axis_at, parts in cuts:
        heights = jax.random.uniform(jax.random.fold_in(jax.random.fold_in(own_key, 6), axis_at), (parts,), jnp.float32, low / len(cuts), top_value / len(cuts))
        factor_of = factor_of * jnp.repeat(jnp.exp(heights), extent[axis_at] // parts).reshape((-1,) + (1,) * (len(extent) - 1 - axis_at))
    return factor_of


def rank_table(count, lean):
    loads = [(1 << 20) // math.isqrt(rank ** lean) + 1 for rank in range(1, count + 1)]
    deviation = 1 + sum(loads) // (1 << 30)
    return np.cumsum(np.array([max(1, weight // deviation) for weight in loads]))


def skewed_ids(key, extent, count, lean):
    table = rank_table(count, lean)
    ticket = jax.random.randint(jax.random.fold_in(key, 1), extent, 0, int(table[count - 1]))
    rank = jnp.searchsorted(jnp.asarray(table, jnp.int32), ticket, side="right")
    return jax.random.permutation(jax.random.fold_in(key, 2), count)[rank].astype(jnp.int32)


def length_profile(number_of, total, limit, slope):
    portions = [(1 << 20) // math.isqrt(rank ** slope) + 1 for rank in range(2, number_of + 1)]
    spare, counts = total - limit - (number_of - 1), [1] * (number_of - 1)
    while spare > 0:
        movable = [i for i in range(number_of - 1) if counts[i] < limit]
        whole, remaining = sum([portions[i] for i in movable]), spare
        for i in movable:
            extra = min(limit - counts[i], max(1, remaining * portions[i] // whole), spare)
            counts[i] = counts[i] + extra
            spare = spare - extra
    return np.array([limit] + counts)


def uneven(key, count, total, reach, lean):
    if count == 2:
        one = jax.random.randint(key, (), max(1, total - reach), min(reach, total - 1) + 1)
        return jnp.stack([one, total - one])
    sizes = jnp.asarray(length_profile(count, total, reach, lean), jnp.int32)
    couples = (count - 1) // 2
    giver, taker = sizes[1:1 + 2 * couples:2], sizes[2:2 + 2 * couples:2]
    margin = jnp.minimum(giver - 1, reach - taker)
    shifted = jax.random.randint(jax.random.fold_in(key, 1), (couples,), 0, 1 << 20) % (margin + 1)
    sizes = sizes.at[1:1 + 2 * couples:2].set(giver - shifted).at[2:2 + 2 * couples:2].set(taker + shifted)
    return sizes[jax.random.permutation(jax.random.fold_in(key, 2), count)]


def bell_draw(key, extent, scale, reach, pieces=(), kind=jnp.bfloat16):
    result = scale * jax.random.normal(key, extent, jnp.float32)
    if pieces:
        result = result * shard_levels(key, extent, pieces, -0.22, 0.18)
    return jnp.clip(result, -reach, reach).astype(kind)


def setup_inputs(seed: int = 0) -> dict:
    keys = jax.random.split(jax.random.key(seed), 9)
    return {
        "activations": bell_draw(keys[0], (TOKENS, D), 1.0, 6.0, ((0, 96), (1, 8))),
        "cotangent": bell_draw(keys[1], (TOKENS, D), (TOKENS ** -0.5), 0.0625, ((0, 96), (1, 8))),
        "factor_down": bell_draw(keys[2], (D, R), D ** -0.5, 0.0625, ((0, 8),), jnp.float32),
        "factor_up": bell_draw(keys[3], (R, D), R ** -0.5, 0.75, ((1, 8),), jnp.float32),
        "first_moment": bell_draw(keys[4], (N_TENSOR, FLAT_PAD), 0.5, 4.0, ((0, 8), (1, 96)), jnp.float32),
        "second_moment": jnp.clip(jnp.exp(math.log(1.0) - 4.6051702 * jax.random.uniform(keys[5], (N_TENSOR, FLAT_PAD), jnp.float32) ** shard_levels(keys[5], (N_TENSOR, FLAT_PAD), ((0, 8), (1, 96)), -0.2, 0.2)), 0.01, 1.0),
        "piece_lengths": jax.vmap(lambda own: uneven(own, SEGS, FLAT_PAD, 2 * FLAT_PAD // SEGS, 2))(jax.random.split(keys[6], N_TENSOR)).reshape((N_TENSOR, SEGS)).astype(jnp.int32),
        "writers": with_ends(skewed_ids(keys[7], (N_TENSOR, SEGS), N_DP, 2), jax.random.fold_in(keys[7], 3), 0, N_DP - 1).astype(jnp.int32),
    }


def flatten_pair(left, right):
    width = left.shape[0] // N_TENSOR
    first = left.reshape(N_TENSOR, width * R)
    second = right.reshape(R, N_TENSOR, width).transpose(1, 0, 2).reshape(N_TENSOR, width * R)
    padding = jnp.zeros((N_TENSOR, FLAT_PAD - 2 * width * R), jnp.float32)
    return jnp.concatenate([first, second, padding], axis=1)

def reference(activations, cotangent, factor_down, factor_up, first_moment, second_moment, piece_lengths, writers):
    down_b = factor_down.astype(jnp.bfloat16)
    up_b = factor_up.astype(jnp.bfloat16)
    width = D // N_TENSOR
    reduced = jnp.zeros((activations.shape[0], R), jnp.float32)
    projected = jnp.zeros((activations.shape[0], R), jnp.float32)
    for rank in range(N_TENSOR):
        lower = rank * width
        upper = lower + width
        part_one = jnp.dot(activations[:, lower:upper], down_b[lower:upper], preferred_element_type=jnp.float32).astype(jnp.bfloat16)
        part_two = jnp.dot(cotangent[:, lower:upper], up_b[:, lower:upper].T, preferred_element_type=jnp.float32).astype(jnp.bfloat16)
        part_one, part_two = lax.optimization_barrier((part_one, part_two))
        reduced = reduced + part_one.astype(jnp.float32)
        projected = projected + part_two.astype(jnp.float32)
    reduced_b = reduced.astype(jnp.bfloat16)
    projected_b = projected.astype(jnp.bfloat16)
    grad_up = 2.0 * jnp.dot(reduced_b.T, cotangent, preferred_element_type=jnp.float32)
    grad_down = 2.0 * jnp.dot(activations.T, projected_b, preferred_element_type=jnp.float32)
    flat_grad = flatten_pair(grad_down, grad_up)
    flat_param = flatten_pair(factor_down, factor_up)
    moment_one = 0.9 * first_moment + 0.1 * flat_grad
    moment_two = 0.999 * second_moment + 0.001 * flat_grad * flat_grad
    fixed_one = 1.0 - 0.9 ** 10
    fixed_two = 1.0 - 0.999 ** 10
    updated = flat_param - 0.01 * (moment_one / fixed_one) / (jnp.sqrt(moment_two / fixed_two) + 1e-08)
    partition = jnp.stack([updated, moment_one, moment_two])
    owner_rows = []
    for rank in range(N_TENSOR):
        owner_rows.append(jnp.repeat(writers[rank], piece_lengths[rank], total_repeat_length=FLAT_PAD))
    owners = jnp.stack(owner_rows)
    ranks = jnp.arange(N_DP, dtype=jnp.int32)
    hits = owners[None, :, :] == ranks[:, None, None]
    written = jnp.where(hits[None], partition[:, None], jnp.float32(0.0))
    return (partition, written)
```

```python
import functools

import jax
import jax.numpy as jnp
from jax import lax
from jax.experimental import pallas as pl
from jax.experimental.pallas import tpu as pltpu
from jax.sharding import Mesh, PartitionSpec as P

BF16 = jnp.bfloat16
F32 = jnp.float32
LANES = 128
VMEM = pl.BlockSpec(memory_space=pltpu.VMEM)
HBM = pl.BlockSpec(memory_space=pltpu.HBM)
SMEM = pl.BlockSpec(memory_space=pltpu.SMEM)
NT = (((1,), (1,)), ((), ()))
PARAMS = pltpu.CompilerParams(vmem_limit_bytes=16 * 1024 * 1024)


def low_rank_kernel(rows, act, cot, down_t, up, first, second, out, packed, a, c, d, u, one, two, sems):
    count = sems.shape[0] // 2 - 2
    tall = act.shape[0] // count
    weights = [pltpu.make_async_copy(down_t, d, sems.at[0]), pltpu.make_async_copy(up, u, sems.at[1])]
    moments = [pltpu.make_async_copy(first, one, sems.at[2]), pltpu.make_async_copy(second, two, sems.at[3])]
    blocks = []
    for i in range(count):
        at = pl.ds(i * tall, tall)
        blocks.append(
            (
                pltpu.make_async_copy(act.at[at], a.at[at], sems.at[4 + 2 * i]),
                pltpu.make_async_copy(cot.at[at], c.at[at], sems.at[5 + 2 * i]),
            )
        )
    for copy in weights + [copy for pair in blocks for copy in pair] + moments:
        copy.start()
    for copy in weights:
        copy.wait()
    down_b = d[...].astype(BF16)
    up_b = u[...].astype(BF16)
    blank = jnp.zeros_like(down_b)
    left = jnp.concatenate([down_b, blank], axis=0)
    right = jnp.concatenate([blank, up_b], axis=0)
    for i, pair in enumerate(blocks):
        at = slice(i * tall, (i + 1) * tall)
        pair[0].wait()
        both = lax.dot_general(a[at], left, NT, preferred_element_type=F32)
        pair[1].wait()
        both += lax.dot_general(c[at], right, NT, preferred_element_type=F32)
        out[at, :] = both.astype(BF16)
    for copy in moments:
        copy.wait()
    half = packed.shape[0] // 2
    packed[...] = jnp.zeros_like(packed)
    for i, source in enumerate((one, two)):
        for r in range(rows):
            packed[half * i + r : half * i + r + 1, :] = source[:, r * LANES : (r + 1) * LANES]


def add_copies_kernel(mine, other, out):
    total = (mine[...].astype(F32) + other[...].astype(F32)).astype(BF16)
    for i in range(out.shape[0]):
        out[i] = total


def store_flat(flat, wide, down_t2, up):
    width = up.shape[1]
    rank = up.shape[0]
    half = width // 2
    per_row = width // LANES
    wide[...] = down_t2.T
    even = wide[pl.ds(0, half, stride=2), :]
    odd = wide[pl.ds(1, half, stride=2), :]
    lane = lax.broadcasted_iota(jnp.int32, (half, LANES), 1)
    flat[0:half, :] = jnp.where(lane < rank, even, odd)
    for c in range(per_row):
        flat[pl.ds(half + c, rank, stride=per_row), :] = up[:, c * LANES : (c + 1) * LANES]
    used = half + rank * per_row
    flat[used:, :] = jnp.zeros((flat.shape[0] - used, LANES), F32)


def param_kernel(down_t, up, flat, wide):
    left = down_t[...]
    store_flat(flat, wide, jnp.concatenate([left, left], axis=0), up[...])


def grad_kernel(rows, parts, act, cot, out, flat, wide):
    total = parts[0].astype(F32)
    for i in range(1, parts.shape[0]):
        total += parts[i].astype(F32)
    turned = total.T.astype(BF16)
    rank = turned.shape[0] // 2
    projected = turned[rank:]
    twice = jnp.concatenate([projected, projected], axis=0)
    up = 2.0 * jnp.dot(turned[:rank], cot[...], preferred_element_type=F32)
    down = 2.0 * jnp.dot(twice, act[...], preferred_element_type=F32)
    store_flat(flat, wide, down, up)
    part = out.shape[1]
    for j in range(out.shape[0]):
        for i in range(out.shape[2] // LANES):
            at = rows * j + part * i
            out[j, :, i * LANES : (i + 1) * LANES] = flat[at : at + part, :].astype(BF16)


def adam(param, grad, moment_one, moment_two):
    fresh_one = moment_one + 0.1 * grad
    fresh_two = moment_two + 0.001 * grad * grad
    fixed_one = 1.0 - 0.9**10
    fixed_two = 1.0 - 0.999**10
    updated = param - 0.01 * (fresh_one / fixed_one) / (jnp.sqrt(fresh_two / fixed_two) + 1e-08)
    return updated, fresh_one, fresh_two


def partition_kernel(rows, me, parts, flat, first, second, out, send, grad, one, two):
    total = jnp.sum(parts[...].astype(F32), axis=0)
    part = total.shape[0]
    for i in range(total.shape[1] // LANES):
        grad[part * i : part * (i + 1), :] = total[:, i * LANES : (i + 1) * LANES]
    packed = total.astype(BF16)
    for j in range(send.shape[0]):
        send[j] = packed
    for r in range(rows):
        one[r : r + 1, :] = first[:, r * LANES : (r + 1) * LANES]
        two[r : r + 1, :] = second[:, r * LANES : (r + 1) * LANES]
    param = flat[pl.ds(me[0] * rows, grad.shape[0]), :]
    fresh = adam(param, grad[...], 0.9 * one[...], 0.999 * two[...])
    for i in range(3):
        for r in range(rows):
            out[i, :, r * LANES : (r + 1) * LANES] = fresh[i][r : r + 1, :]


def prepare_kernel(rows, me, lengths, writers, packed, one, two, mask):
    mask[...] = jnp.zeros_like(mask)
    block = 8 * LANES
    spot = lax.broadcasted_iota(jnp.int32, (8, LANES), 0) * LANES + lax.broadcasted_iota(
        jnp.int32, (8, LANES), 1
    )

    def piece(k, start):
        end = start + lengths[0, k]

        @pl.when(writers[0, k] == me[0])
        def _():
            def mark(b, carry):
                here = spot + b * block
                at = pl.ds(pl.multiple_of(b * 8, 8), 8)
                inside = jnp.logical_and(here >= start, here < end)
                mask[at, :] = jnp.where(inside, 1.0, mask[at, :])
                return carry

            lax.fori_loop(start // block, (end + block - 1) // block, mark, 0)

        return end

    lax.fori_loop(0, lengths.shape[1], piece, 0)
    count = one.shape[0] // rows
    half = packed.shape[0] // count // 2
    for j in range(count):
        base = 2 * half * j
        tall = min(half, one.shape[0] - rows * j)
        one[rows * j : rows * j + tall, :] = 0.9 * packed[base : base + tall, :]
        two[rows * j : rows * j + tall, :] = 0.999 * packed[base + half : base + half + tall, :]


def written_kernel(rows, grads, first, second, flat, mask, out, grad, fresh, sems):
    part = grads.shape[1]
    steps = sems.shape[0]
    per_step = grads.shape[0] // steps
    tall = per_step * rows
    copies = []
    for s in range(steps):
        for j in range(s * per_step, (s + 1) * per_step):
            for i in range(grads.shape[2] // LANES):
                at = rows * j + part * i
                grad[at : at + part, :] = grads[j, :, i * LANES : (i + 1) * LANES].astype(F32)
        for r in range(s * tall, (s + 1) * tall, 24):
            at = slice(r, r + 24)
            keep = mask[at, :] > 0.0
            values = adam(flat[at, :], grad[at, :], first[at, :], second[at, :])
            for i in range(3):
                fresh[i, at, :] = jnp.where(keep, values[i], 0.0)
        block = pl.ds(s * tall, tall)
        copies.append(pltpu.make_async_copy(fresh.at[:, block], out.at[:, block], sems.at[s]))
        copies[-1].start()
    for copy in copies:
        copy.wait()


def gather_moments(packed, dp):
    return lax.all_gather(packed, dp, axis=0, tiled=True)


def body(dp, activations, cotangent, factor_down, factor_up, first_moment, second_moment, piece_lengths, writers):
    dp_count = lax.axis_size(dp)
    part_len = first_moment.shape[1]
    rows = part_len // LANES
    all_rows = rows * dp_count
    part = 4
    lanes = -(-rows // part) * LANES
    tokens, width = activations.shape
    rank = factor_up.shape[0]
    me = lax.axis_index(dp).astype(jnp.int32).reshape(1)
    down_t = factor_down.T
    x_count = lax.axis_size("x")

    blocks = 4
    partial, packed = pl.pallas_call(
        functools.partial(low_rank_kernel, rows),
        out_shape=(
            jax.ShapeDtypeStruct((tokens, 2 * rank), BF16),
            jax.ShapeDtypeStruct((24, LANES), F32),
        ),
        in_specs=[HBM] * 6,
        out_specs=(VMEM, VMEM),
        scratch_shapes=[
            pltpu.VMEM((tokens, width), BF16),
            pltpu.VMEM((tokens, width), BF16),
            pltpu.VMEM((rank, width), F32),
            pltpu.VMEM((rank, width), F32),
            pltpu.VMEM((1, part_len), F32),
            pltpu.VMEM((1, part_len), F32),
            pltpu.SemaphoreType.DMA((4 + 2 * blocks,)),
        ],
        compiler_params=pltpu.CompilerParams(vmem_limit_bytes=56 * 1024 * 1024),
        name="low_rank",
    )(activations, cotangent, down_t, factor_up, first_moment, second_moment)
    all_moments = gather_moments(packed, dp)
    other = lax.ppermute(partial, "c", [(0, 1), (1, 0)])
    flat_param = pl.pallas_call(
        param_kernel,
        out_shape=jax.ShapeDtypeStruct((all_rows + 8, LANES), F32),
        in_specs=[VMEM] * 2,
        out_specs=VMEM,
        scratch_shapes=[pltpu.VMEM((width, LANES), F32)],
        compiler_params=PARAMS,
        name="flat_param",
    )(down_t, factor_up)
    copies = pl.pallas_call(
        add_copies_kernel,
        out_shape=jax.ShapeDtypeStruct((x_count, tokens, 2 * rank), BF16),
        in_specs=[VMEM] * 2,
        out_specs=VMEM,
        compiler_params=PARAMS,
        name="add_cores",
    )(partial, other)
    parts = lax.all_to_all(copies, "x", 0, 0)
    chunks = pl.pallas_call(
        functools.partial(grad_kernel, rows),
        out_shape=jax.ShapeDtypeStruct((dp_count, part, lanes), BF16),
        in_specs=[VMEM] * 3,
        out_specs=VMEM,
        scratch_shapes=[
            pltpu.VMEM((all_rows + 8, LANES), F32),
            pltpu.VMEM((width, LANES), F32),
        ],
        compiler_params=PARAMS,
        name="grads",
    )(parts, activations, cotangent)
    mine = lax.all_to_all(chunks, dp, 0, 0)
    partition, send = pl.pallas_call(
        functools.partial(partition_kernel, rows),
        out_shape=(
            jax.ShapeDtypeStruct((3, 1, part_len), F32),
            jax.ShapeDtypeStruct((dp_count, part, lanes), BF16),
        ),
        in_specs=[SMEM] + [VMEM] * 4,
        out_specs=(VMEM, VMEM),
        scratch_shapes=[pltpu.VMEM((lanes * part // LANES, LANES), F32)] * 3,
        compiler_params=PARAMS,
        name="partition",
    )(me, mine, flat_param, first_moment, second_moment)
    grads = lax.all_to_all(send, dp, 0, 0)
    one, two, mask = pl.pallas_call(
        functools.partial(prepare_kernel, rows),
        out_shape=[jax.ShapeDtypeStruct((all_rows, LANES), F32)] * 3,
        in_specs=[SMEM] * 3 + [VMEM],
        out_specs=[VMEM] * 3,
        compiler_params=PARAMS,
        name="prepare",
    )(me, piece_lengths, writers, all_moments)
    written = pl.pallas_call(
        functools.partial(written_kernel, rows),
        out_shape=jax.ShapeDtypeStruct((3, all_rows, LANES), F32),
        in_specs=[VMEM] * 5,
        out_specs=HBM,
        scratch_shapes=[
            pltpu.VMEM((all_rows + 8, LANES), F32),
            pltpu.VMEM((3, all_rows, LANES), F32),
            pltpu.SemaphoreType.DMA((4,)),
        ],
        compiler_params=PARAMS,
        name="written",
    )(grads, one, two, flat_param, mask)
    return (partition, written.reshape(3, 1, 1, all_rows * LANES))


def solution(mesh):
    fine = Mesh(mesh.devices.reshape(8, 12, 4, 2), ("y", "z", "x", "c"))
    return on_mesh(fine)


def on_mesh(fine):
    dp, tensor = ("y", "z"), ("x", "c")
    in_specs = (
        P(dp, tensor),
        P(dp, tensor),
        P(tensor, None),
        P(None, tensor),
        P(tensor, dp),
        P(tensor, dp),
        P(tensor, None),
        P(tensor, None),
    )
    out_specs = (P(None, tensor, dp), P(None, dp, tensor, None))
    return jax.shard_map(
        functools.partial(body, dp), mesh=fine, in_specs=in_specs, out_specs=out_specs, check_vma=False
    )
```

```python
import functools

import jax
import jax.numpy as jnp
from jax import lax
from jax.experimental import pallas as pl
from jax.experimental.pallas import tpu as pltpu
from jax.sharding import Mesh, PartitionSpec as P

BF16 = jnp.bfloat16
F32 = jnp.float32
LANES = 128
VMEM = pl.BlockSpec(memory_space=pltpu.VMEM)
HBM = pl.BlockSpec(memory_space=pltpu.HBM)
SMEM = pl.BlockSpec(memory_space=pltpu.SMEM)
NT = (((1,), (1,)), ((), ()))
PARAMS = pltpu.CompilerParams(vmem_limit_bytes=16 * 1024 * 1024)


def low_rank_kernel(act, cot, down_t, up, out, a, c, d, u, sems):
    copies = [
        pltpu.make_async_copy(source, target, sems.at[i])
        for i, (source, target) in enumerate(((down_t, d), (act, a), (up, u), (cot, c)))
    ]
    for copy in copies:
        copy.start()
    copies[0].wait()
    down_b = d[...].astype(BF16)
    blank = jnp.zeros_like(down_b)
    left = jnp.concatenate([down_b, blank], axis=0)
    copies[1].wait()
    both = lax.dot_general(a[...], left, NT, preferred_element_type=F32)
    copies[2].wait()
    right = jnp.concatenate([blank, u[...].astype(BF16)], axis=0)
    copies[3].wait()
    both += lax.dot_general(c[...], right, NT, preferred_element_type=F32)
    out[...] = both.astype(BF16)


def add_copies_kernel(mine, other, out):
    total = (mine[...].astype(F32) + other[...].astype(F32)).astype(BF16)
    for i in range(out.shape[0]):
        out[i] = total


def store_flat(flat, wide, down_t2, up):
    width = up.shape[1]
    rank = up.shape[0]
    half = width // 2
    per_row = width // LANES
    wide[...] = down_t2.T
    even = wide[pl.ds(0, half, stride=2), :]
    odd = wide[pl.ds(1, half, stride=2), :]
    lane = lax.broadcasted_iota(jnp.int32, (half, LANES), 1)
    flat[0:half, :] = jnp.where(lane < rank, even, odd)
    for c in range(per_row):
        flat[pl.ds(half + c, rank, stride=per_row), :] = up[:, c * LANES : (c + 1) * LANES]
    used = half + rank * per_row
    flat[used:, :] = jnp.zeros((flat.shape[0] - used, LANES), F32)


def param_kernel(me, lengths, writers, down_t, up, flat, mask, wide):
    left = down_t[...]
    store_flat(flat, wide, jnp.concatenate([left, left], axis=0), up[...])
    mask[...] = jnp.zeros_like(mask)
    block = 8 * LANES
    spot = lax.broadcasted_iota(jnp.int32, (8, LANES), 0) * LANES + lax.broadcasted_iota(
        jnp.int32, (8, LANES), 1
    )

    def piece(k, start):
        end = start + lengths[0, k]

        @pl.when(writers[0, k] == me[0])
        def _():
            def mark(b, carry):
                here = spot + b * block
                at = pl.ds(pl.multiple_of(b * 8, 8), 8)
                inside = jnp.logical_and(here >= start, here < end)
                mask[at, :] = jnp.where(inside, 1.0, mask[at, :])
                return carry

            lax.fori_loop(start // block, (end + block - 1) // block, mark, 0)

        return end

    lax.fori_loop(0, lengths.shape[1], piece, 0)


def grad_kernel(rows, parts, act, cot, out, flat, wide):
    total = parts[0].astype(F32)
    for i in range(1, parts.shape[0]):
        total += parts[i].astype(F32)
    turned = total.T.astype(BF16)
    rank = turned.shape[0] // 2
    projected = turned[rank:]
    twice = jnp.concatenate([projected, projected], axis=0)
    up = 2.0 * jnp.dot(turned[:rank], cot[...], preferred_element_type=F32)
    down = 2.0 * jnp.dot(twice, act[...], preferred_element_type=F32)
    store_flat(flat, wide, down, up)
    part = out.shape[1]
    for j in range(out.shape[0]):
        for i in range(out.shape[2] // LANES):
            at = rows * j + part * i
            out[j, :, i * LANES : (i + 1) * LANES] = flat[at : at + part, :].astype(BF16)


def adam_moments(grad, moment_one, moment_two):
    return 0.9 * moment_one + 0.1 * grad, 0.999 * moment_two + 0.001 * grad * grad


def adam_param(param, fresh_one, fresh_two):
    fixed_one = 1.0 - 0.9**10
    fixed_two = 1.0 - 0.999**10
    return param - 0.01 * (fresh_one / fixed_one) / (jnp.sqrt(fresh_two / fixed_two) + 1e-08)


def partition_kernel(rows, me, parts, flat, first, second, out, send, grad, one, two):
    total = jnp.sum(parts[...].astype(F32), axis=0)
    part = total.shape[0]
    half = grad.shape[0]
    for i in range(total.shape[1] // LANES):
        grad[part * i : part * (i + 1), :] = total[:, i * LANES : (i + 1) * LANES]
    for r in range(rows):
        one[r : r + 1, :] = first[:, r * LANES : (r + 1) * LANES]
        two[r : r + 1, :] = second[:, r * LANES : (r + 1) * LANES]
    blank = jnp.zeros((half - rows, LANES), F32)
    one[rows:, :] = blank
    two[rows:, :] = blank
    fresh = adam_moments(grad[...], one[...], two[...])
    both = jnp.concatenate(fresh, axis=0).astype(BF16)
    for j in range(send.shape[0]):
        send[j] = both
    updated = adam_param(flat[pl.ds(me[0] * rows, half), :], *fresh)
    for i, values in enumerate((updated,) + fresh):
        for r in range(rows):
            out[i, :, r * LANES : (r + 1) * LANES] = values[r : r + 1, :]


def copies_kernel(source, out):
    values = source[...]
    for i in range(out.shape[0]):
        out[i] = values


def written_kernel(rows, moments, flat, mask, out, one, two, fresh, sems):
    half = moments.shape[1] // 2
    steps = sems.shape[0]
    per_step = moments.shape[0] // steps
    tall = per_step * rows
    copies = []
    for s in range(steps):
        for j in range(s * per_step, (s + 1) * per_step):
            values = moments[j].astype(F32)
            one[rows * j : rows * j + half, :] = values[:half]
            two[rows * j : rows * j + half, :] = values[half:]
        for r in range(s * tall, (s + 1) * tall, 24):
            at = slice(r, r + 24)
            keep = mask[at, :] > 0.0
            fresh_one, fresh_two = one[at, :], two[at, :]
            updated = adam_param(flat[at, :], fresh_one, fresh_two)
            for i, values in enumerate((updated, fresh_one, fresh_two)):
                fresh[i, at, :] = jnp.where(keep, values, 0.0)
        block = pl.ds(s * tall, tall)
        copies.append(pltpu.make_async_copy(fresh.at[:, block], out.at[:, block], sems.at[s]))
        copies[-1].start()
    for copy in copies:
        copy.wait()


def body(dp, activations, cotangent, factor_down, factor_up, first_moment, second_moment, piece_lengths, writers):
    dp_count = lax.axis_size(dp)
    part_len = first_moment.shape[1]
    rows = part_len // LANES
    all_rows = rows * dp_count
    part = 4
    lanes = -(-rows // part) * LANES
    tokens, width = activations.shape
    rank = factor_up.shape[0]
    me = lax.axis_index(dp).astype(jnp.int32).reshape(1)
    down_t = factor_down.T
    x_count = lax.axis_size("x")

    partial, act_copy, cot_copy = pl.pallas_call(
        low_rank_kernel,
        out_shape=(
            jax.ShapeDtypeStruct((tokens, 2 * rank), BF16),
            jax.ShapeDtypeStruct((tokens, width), BF16),
            jax.ShapeDtypeStruct((tokens, width), BF16),
        ),
        in_specs=[HBM] * 4,
        out_specs=(VMEM, VMEM, VMEM),
        scratch_shapes=[
            pltpu.VMEM((rank, width), F32),
            pltpu.VMEM((rank, width), F32),
            pltpu.SemaphoreType.DMA((4,)),
        ],
        compiler_params=PARAMS,
        name="low_rank",
    )(*[pltpu.with_memory_space_constraint(v, pltpu.HBM) for v in (activations, cotangent, down_t, factor_up)])
    other = lax.ppermute(partial, "c", [(0, 1), (1, 0)])
    flat_param, mask = pl.pallas_call(
        param_kernel,
        out_shape=(
            jax.ShapeDtypeStruct((all_rows + 8, LANES), F32),
            jax.ShapeDtypeStruct((all_rows, LANES), F32),
        ),
        in_specs=[SMEM] * 3 + [VMEM] * 2,
        out_specs=(VMEM, VMEM),
        scratch_shapes=[pltpu.VMEM((width, LANES), F32)],
        compiler_params=PARAMS,
        name="flat_param",
    )(me, piece_lengths, writers, down_t, factor_up)
    copies = pl.pallas_call(
        add_copies_kernel,
        out_shape=jax.ShapeDtypeStruct((x_count, tokens, 2 * rank), BF16),
        in_specs=[VMEM] * 2,
        out_specs=VMEM,
        compiler_params=PARAMS,
        name="add_cores",
    )(partial, other)
    parts = lax.all_to_all(copies, "x", 0, 0)
    chunks = pl.pallas_call(
        functools.partial(grad_kernel, rows),
        out_shape=jax.ShapeDtypeStruct((dp_count, part, lanes), BF16),
        in_specs=[VMEM] * 3,
        out_specs=VMEM,
        scratch_shapes=[
            pltpu.VMEM((all_rows + 8, LANES), F32),
            pltpu.VMEM((width, LANES), F32),
        ],
        compiler_params=PARAMS,
        name="grads",
    )(parts, act_copy, cot_copy)
    mine = lax.all_to_all(chunks, dp, 0, 0)
    half = lanes * part // LANES
    z_count = lax.axis_size(dp[1])
    partition, send = pl.pallas_call(
        functools.partial(partition_kernel, rows),
        out_shape=(
            jax.ShapeDtypeStruct((3, 1, part_len), F32),
            jax.ShapeDtypeStruct((z_count, 2 * half, LANES), BF16),
        ),
        in_specs=[SMEM] + [VMEM] * 4,
        out_specs=(VMEM, VMEM),
        scratch_shapes=[pltpu.VMEM((half, LANES), F32)] * 3,
        compiler_params=PARAMS,
        name="partition",
    )(me, mine, flat_param, first_moment, second_moment)
    row = lax.all_to_all(send, dp[1], 0, 0)
    row_copies = pl.pallas_call(
        copies_kernel,
        out_shape=jax.ShapeDtypeStruct((lax.axis_size(dp[0]), z_count * 2 * half, LANES), BF16),
        in_specs=[VMEM],
        out_specs=VMEM,
        compiler_params=PARAMS,
        name="row_copies",
    )(row.reshape(z_count * 2 * half, LANES))
    moments = lax.all_to_all(row_copies, dp[0], 0, 0)
    written = pl.pallas_call(
        functools.partial(written_kernel, rows),
        out_shape=jax.ShapeDtypeStruct((3, all_rows, LANES), F32),
        in_specs=[VMEM] * 3,
        out_specs=HBM,
        scratch_shapes=[
            pltpu.VMEM((all_rows + 8, LANES), F32),
            pltpu.VMEM((all_rows + 8, LANES), F32),
            pltpu.VMEM((3, all_rows, LANES), F32),
            pltpu.SemaphoreType.DMA((4,)),
        ],
        compiler_params=PARAMS,
        name="written",
    )(moments.reshape(dp_count, 2 * half, LANES), flat_param, mask)
    return (partition, written.reshape(3, 1, 1, all_rows * LANES))


def solution(mesh):
    fine = Mesh(mesh.devices.reshape(8, 12, 4, 2), ("y", "z", "x", "c"))
    return on_mesh(fine)


def on_mesh(fine):
    dp, tensor = ("y", "z"), ("x", "c")
    in_specs = (
        P(dp, tensor),
        P(dp, tensor),
        P(tensor, None),
        P(None, tensor),
        P(tensor, dp),
        P(tensor, dp),
        P(tensor, None),
        P(tensor, None),
    )
    out_specs = (P(None, tensor, dp), P(None, dp, tensor, None))
    return jax.shard_map(
        functools.partial(body, dp), mesh=fine, in_specs=in_specs, out_specs=out_specs, check_vma=False
    )
```

```python
import functools

import jax
import jax.numpy as jnp
from jax import lax
from jax.experimental import pallas as pl
from jax.experimental.pallas import tpu as pltpu
from jax.sharding import Mesh, PartitionSpec as P

BF16 = jnp.bfloat16
F32 = jnp.float32
LANES = 128
VMEM = pl.BlockSpec(memory_space=pltpu.VMEM)
HBM = pl.BlockSpec(memory_space=pltpu.HBM)
SMEM = pl.BlockSpec(memory_space=pltpu.SMEM)
NT = (((1,), (1,)), ((), ()))
PARAMS = pltpu.CompilerParams(vmem_limit_bytes=16 * 1024 * 1024)


def low_rank_kernel(act, cot, down_t, up, out, a, c, d, u, sems):
    copies = [
        pltpu.make_async_copy(source, target, sems.at[i])
        for i, (source, target) in enumerate(((down_t, d), (act, a), (up, u), (cot, c)))
    ]
    for copy in copies:
        copy.start()
    copies[0].wait()
    down_b = d[...].astype(BF16)
    blank = jnp.zeros_like(down_b)
    left = jnp.concatenate([down_b, blank], axis=0)
    copies[1].wait()
    both = lax.dot_general(a[...], left, NT, preferred_element_type=F32)
    copies[2].wait()
    right = jnp.concatenate([blank, u[...].astype(BF16)], axis=0)
    copies[3].wait()
    both += lax.dot_general(c[...], right, NT, preferred_element_type=F32)
    out[...] = both.astype(BF16)


def add_copies_kernel(mine, other, out):
    total = (mine[...].astype(F32) + other[...].astype(F32)).astype(BF16)
    for i in range(out.shape[0]):
        out[i] = total


def store_flat(flat, wide, down_t2, up):
    width = up.shape[1]
    rank = up.shape[0]
    half = width // 2
    per_row = width // LANES
    wide[...] = down_t2.T
    even = wide[pl.ds(0, half, stride=2), :]
    odd = wide[pl.ds(1, half, stride=2), :]
    lane = lax.broadcasted_iota(jnp.int32, (half, LANES), 1)
    flat[0:half, :] = jnp.where(lane < rank, even, odd)
    for c in range(per_row):
        flat[pl.ds(half + c, rank, stride=per_row), :] = up[:, c * LANES : (c + 1) * LANES]
    used = half + rank * per_row
    flat[used:, :] = jnp.zeros((flat.shape[0] - used, LANES), F32)


def param_kernel(me, lengths, writers, down_t, up, flat, mask, wide):
    left = down_t[...]
    store_flat(flat, wide, jnp.concatenate([left, left], axis=0), up[...])
    mask[...] = jnp.zeros_like(mask)
    block = 8 * LANES
    spot = lax.broadcasted_iota(jnp.int32, (8, LANES), 0) * LANES + lax.broadcasted_iota(
        jnp.int32, (8, LANES), 1
    )

    def piece(k, start):
        end = start + lengths[0, k]

        @pl.when(writers[0, k] == me[0])
        def _():
            def mark(b, carry):
                here = spot + b * block
                at = pl.ds(pl.multiple_of(b * 8, 8), 8)
                inside = jnp.logical_and(here >= start, here < end)
                mask[at, :] = jnp.where(inside, 1.0, mask[at, :])
                return carry

            lax.fori_loop(start // block, (end + block - 1) // block, mark, 0)

        return end

    lax.fori_loop(0, lengths.shape[1], piece, 0)


def grad_kernel(rows, parts, act, cot, out, flat, wide):
    total = parts[0].astype(F32)
    for i in range(1, parts.shape[0]):
        total += parts[i].astype(F32)
    turned = total.T.astype(BF16)
    rank = turned.shape[0] // 2
    projected = turned[rank:]
    twice = jnp.concatenate([projected, projected], axis=0)
    up = 2.0 * jnp.dot(turned[:rank], cot[...], preferred_element_type=F32)
    down = 2.0 * jnp.dot(twice, act[...], preferred_element_type=F32)
    store_flat(flat, wide, down, up)
    part = out.shape[1]
    for j in range(out.shape[0]):
        for i in range(out.shape[2] // LANES):
            at = rows * j + part * i
            out[j, :, i * LANES : (i + 1) * LANES] = flat[at : at + part, :].astype(BF16)


def adam_moments(grad, moment_one, moment_two):
    return 0.9 * moment_one + 0.1 * grad, 0.999 * moment_two + 0.001 * grad * grad


def adam_param(param, fresh_one, fresh_two):
    fixed_one = 1.0 - 0.9**10
    fixed_two = 1.0 - 0.999**10
    return param - 0.01 * (fresh_one / fixed_one) / (jnp.sqrt(fresh_two / fixed_two) + 1e-08)


def partition_kernel(rows, me, parts, flat, first, second, out, send, grad, one, two, both):
    total = jnp.sum(parts[...].astype(F32), axis=0)
    part = total.shape[0]
    half = grad.shape[0]
    for i in range(total.shape[1] // LANES):
        grad[part * i : part * (i + 1), :] = total[:, i * LANES : (i + 1) * LANES]
    for r in range(rows):
        one[r : r + 1, :] = first[:, r * LANES : (r + 1) * LANES]
        two[r : r + 1, :] = second[:, r * LANES : (r + 1) * LANES]
    blank = jnp.zeros((half - rows, LANES), F32)
    one[rows:, :] = blank
    two[rows:, :] = blank
    fresh = adam_moments(grad[...], one[...], two[...])
    for i in range(2):
        for r in range(rows):
            both[i : i + 1, r * LANES : (r + 1) * LANES] = fresh[i][r : r + 1, :]
    packed = both[...].astype(BF16)
    for j in range(send.shape[0]):
        send[j] = packed
    updated = adam_param(flat[pl.ds(me[0] * rows, half), :], *fresh)
    for i, values in enumerate((updated,) + fresh):
        for r in range(rows):
            out[i, :, r * LANES : (r + 1) * LANES] = values[r : r + 1, :]


def row_kernel(source, out, wide):
    count = source.shape[0]
    for z in range(count):
        pair = source[z].astype(F32)
        for i in range(2):
            wide[i * count + z : i * count + z + 1, :] = pair[i : i + 1]
    values = wide[...].astype(BF16)
    for y in range(out.shape[0]):
        out[y] = values


def written_kernel(rows, moments, flat, mask, out, one, two, fresh, sems):
    count = moments.shape[1] // 2
    steps = sems.shape[0]
    per_step = moments.shape[0] // steps
    tall = per_step * count * rows
    copies = []
    for s in range(steps):
        for y in range(s * per_step, (s + 1) * per_step):
            for r in range(rows):
                values = moments[y, :, r * LANES : (r + 1) * LANES].astype(F32)
                at = pl.ds(y * count * rows + r, count, stride=rows)
                one[at, :] = values[:count]
                two[at, :] = values[count:]
        for r in range(s * tall, (s + 1) * tall, 24):
            at = slice(r, r + 24)
            keep = mask[at, :] > 0.0
            fresh_one, fresh_two = one[at, :], two[at, :]
            updated = adam_param(flat[at, :], fresh_one, fresh_two)
            for i, values in enumerate((updated, fresh_one, fresh_two)):
                fresh[i, at, :] = jnp.where(keep, values, 0.0)
        block = pl.ds(s * tall, tall)
        copies.append(pltpu.make_async_copy(fresh.at[:, block], out.at[:, block], sems.at[s]))
        copies[-1].start()
    for copy in copies:
        copy.wait()


def body(dp, activations, cotangent, factor_down, factor_up, first_moment, second_moment, piece_lengths, writers):
    dp_count = lax.axis_size(dp)
    part_len = first_moment.shape[1]
    rows = part_len // LANES
    all_rows = rows * dp_count
    part = 4
    lanes = -(-rows // part) * LANES
    tokens, width = activations.shape
    rank = factor_up.shape[0]
    me = lax.axis_index(dp).astype(jnp.int32).reshape(1)
    down_t = factor_down.T
    x_count = lax.axis_size("x")

    partial, act_copy, cot_copy = pl.pallas_call(
        low_rank_kernel,
        out_shape=(
            jax.ShapeDtypeStruct((tokens, 2 * rank), BF16),
            jax.ShapeDtypeStruct((tokens, width), BF16),
            jax.ShapeDtypeStruct((tokens, width), BF16),
        ),
        in_specs=[HBM] * 4,
        out_specs=(VMEM, VMEM, VMEM),
        scratch_shapes=[
            pltpu.VMEM((rank, width), F32),
            pltpu.VMEM((rank, width), F32),
            pltpu.SemaphoreType.DMA((4,)),
        ],
        compiler_params=PARAMS,
        name="low_rank",
    )(*[pltpu.with_memory_space_constraint(v, pltpu.HBM) for v in (activations, cotangent, down_t, factor_up)])
    other = lax.ppermute(partial, "c", [(0, 1), (1, 0)])
    flat_param, mask = pl.pallas_call(
        param_kernel,
        out_shape=(
            jax.ShapeDtypeStruct((all_rows + 8, LANES), F32),
            jax.ShapeDtypeStruct((all_rows, LANES), F32),
        ),
        in_specs=[SMEM] * 3 + [VMEM] * 2,
        out_specs=(VMEM, VMEM),
        scratch_shapes=[pltpu.VMEM((width, LANES), F32)],
        compiler_params=PARAMS,
        name="flat_param",
    )(me, piece_lengths, writers, down_t, factor_up)
    copies = pl.pallas_call(
        add_copies_kernel,
        out_shape=jax.ShapeDtypeStruct((x_count, tokens, 2 * rank), BF16),
        in_specs=[VMEM] * 2,
        out_specs=VMEM,
        compiler_params=PARAMS,
        name="add_cores",
    )(partial, other)
    parts = lax.all_to_all(copies, "x", 0, 0)
    chunks = pl.pallas_call(
        functools.partial(grad_kernel, rows),
        out_shape=jax.ShapeDtypeStruct((dp_count, part, lanes), BF16),
        in_specs=[VMEM] * 3,
        out_specs=VMEM,
        scratch_shapes=[
            pltpu.VMEM((all_rows + 8, LANES), F32),
            pltpu.VMEM((width, LANES), F32),
        ],
        compiler_params=PARAMS,
        name="grads",
    )(parts, act_copy, cot_copy)
    mine = lax.all_to_all(chunks, dp, 0, 0)
    half = lanes * part // LANES
    z_count = lax.axis_size(dp[1])
    partition, send = pl.pallas_call(
        functools.partial(partition_kernel, rows),
        out_shape=(
            jax.ShapeDtypeStruct((3, 1, part_len), F32),
            jax.ShapeDtypeStruct((z_count, 2, part_len), BF16),
        ),
        in_specs=[SMEM] + [VMEM] * 4,
        out_specs=(VMEM, VMEM),
        scratch_shapes=[pltpu.VMEM((half, LANES), F32)] * 3 + [pltpu.VMEM((2, part_len), F32)],
        compiler_params=PARAMS,
        name="partition",
    )(me, mine, flat_param, first_moment, second_moment)
    row = lax.all_to_all(send, dp[1], 0, 0)
    row_copies = pl.pallas_call(
        row_kernel,
        out_shape=jax.ShapeDtypeStruct((lax.axis_size(dp[0]), 2 * z_count, part_len), BF16),
        in_specs=[VMEM],
        out_specs=VMEM,
        scratch_shapes=[pltpu.VMEM((2 * z_count, part_len), F32)],
        compiler_params=PARAMS,
        name="row_copies",
    )(row)
    moments = lax.all_to_all(row_copies, dp[0], 0, 0)
    written = pl.pallas_call(
        functools.partial(written_kernel, rows),
        out_shape=jax.ShapeDtypeStruct((3, all_rows, LANES), F32),
        in_specs=[VMEM] * 3,
        out_specs=HBM,
        scratch_shapes=[
            pltpu.VMEM((all_rows, LANES), F32),
            pltpu.VMEM((all_rows, LANES), F32),
            pltpu.VMEM((3, all_rows, LANES), F32),
            pltpu.SemaphoreType.DMA((4,)),
        ],
        compiler_params=PARAMS,
        name="written",
    )(moments, flat_param, mask)
    return (partition, written.reshape(3, 1, 1, all_rows * LANES))


def solution(mesh):
    fine = Mesh(mesh.devices.reshape(8, 12, 4, 2), ("y", "z", "x", "c"))
    return on_mesh(fine)


def on_mesh(fine):
    dp, tensor = ("y", "z"), ("x", "c")
    in_specs = (
        P(dp, tensor),
        P(dp, tensor),
        P(tensor, None),
        P(None, tensor),
        P(tensor, dp),
        P(tensor, dp),
        P(tensor, None),
        P(tensor, None),
    )
    out_specs = (P(None, tensor, dp), P(None, dp, tensor, None))
    return jax.shard_map(
        functools.partial(body, dp), mesh=fine, in_specs=in_specs, out_specs=out_specs, check_vma=False
    )
```

```python
import functools

import jax
import jax.numpy as jnp
from jax import lax
from jax.experimental import pallas as pl
from jax.experimental.pallas import tpu as pltpu
from jax.sharding import Mesh, PartitionSpec as P

BF16 = jnp.bfloat16
F32 = jnp.float32
LANES = 128
VMEM = pl.BlockSpec(memory_space=pltpu.VMEM)
HBM = pl.BlockSpec(memory_space=pltpu.HBM)
SMEM = pl.BlockSpec(memory_space=pltpu.SMEM)
NT = (((1,), (1,)), ((), ()))
PARAMS = pltpu.CompilerParams(vmem_limit_bytes=16 * 1024 * 1024)


def low_rank_kernel(act, cot, down_t, up, out, a, c, d, u, sems):
    copies = [
        pltpu.make_async_copy(source, target, sems.at[i])
        for i, (source, target) in enumerate(((down_t, d), (act, a), (up, u), (cot, c)))
    ]
    for copy in copies:
        copy.start()
    copies[0].wait()
    down_b = d[...].astype(BF16)
    blank = jnp.zeros_like(down_b)
    left = jnp.concatenate([down_b, blank], axis=0)
    copies[1].wait()
    both = lax.dot_general(a[...], left, NT, preferred_element_type=F32)
    copies[2].wait()
    right = jnp.concatenate([blank, u[...].astype(BF16)], axis=0)
    copies[3].wait()
    both += lax.dot_general(c[...], right, NT, preferred_element_type=F32)
    out[...] = both.astype(BF16)


def add_copies_kernel(mine, other, after, out):
    total = (mine[...].astype(F32) + other[...].astype(F32)).astype(BF16)
    for i in range(out.shape[0]):
        out[i] = total


def store_flat(flat, wide, down_t2, up):
    width = up.shape[1]
    rank = up.shape[0]
    half = width // 2
    per_row = width // LANES
    wide[...] = down_t2.T
    even = wide[pl.ds(0, half, stride=2), :]
    odd = wide[pl.ds(1, half, stride=2), :]
    lane = lax.broadcasted_iota(jnp.int32, (half, LANES), 1)
    flat[0:half, :] = jnp.where(lane < rank, even, odd)
    for c in range(per_row):
        flat[pl.ds(half + c, rank, stride=per_row), :] = up[:, c * LANES : (c + 1) * LANES]
    used = half + rank * per_row
    flat[used:, :] = jnp.zeros((flat.shape[0] - used, LANES), F32)


def param_kernel(me, lengths, writers, down_t, up, flat, mask, wide):
    left = down_t[...]
    store_flat(flat, wide, jnp.concatenate([left, left], axis=0), up[...])
    mask[...] = jnp.zeros_like(mask)
    block = 8 * LANES
    spot = lax.broadcasted_iota(jnp.int32, (8, LANES), 0) * LANES + lax.broadcasted_iota(
        jnp.int32, (8, LANES), 1
    )

    def piece(k, start):
        end = start + lengths[0, k]

        @pl.when(writers[0, k] == me[0])
        def _():
            def mark(b, carry):
                here = spot + b * block
                at = pl.ds(pl.multiple_of(b * 8, 8), 8)
                inside = jnp.logical_and(here >= start, here < end)
                mask[at, :] = jnp.where(inside, 1.0, mask[at, :])
                return carry

            lax.fori_loop(start // block, (end + block - 1) // block, mark, 0)

        return end

    lax.fori_loop(0, lengths.shape[1], piece, 0, unroll=8)


def grad_kernel(rows, parts, act, cot, out, flat, wide):
    total = parts[0].astype(F32)
    for i in range(1, parts.shape[0]):
        total += parts[i].astype(F32)
    turned = total.T.astype(BF16)
    rank = turned.shape[0] // 2
    projected = turned[rank:]
    twice = jnp.concatenate([projected, projected], axis=0)
    up = 2.0 * jnp.dot(turned[:rank], cot[...], preferred_element_type=F32)
    down = 2.0 * jnp.dot(twice, act[...], preferred_element_type=F32)
    store_flat(flat, wide, down, up)
    part = out.shape[1]
    for j in range(out.shape[0]):
        for i in range(out.shape[2] // LANES):
            at = rows * j + part * i
            out[j, :, i * LANES : (i + 1) * LANES] = flat[at : at + part, :].astype(BF16)


def adam_moments(grad, moment_one, moment_two):
    return 0.9 * moment_one + 0.1 * grad, 0.999 * moment_two + 0.001 * grad * grad


def adam_param(param, fresh_one, fresh_two):
    fixed_one = 1.0 - 0.9**10
    fixed_two = 1.0 - 0.999**10
    return param - 0.01 * (fresh_one / fixed_one) / (jnp.sqrt(fresh_two / fixed_two) + 1e-08)


def own_moments(rows, first, second, one, two):
    for r in range(rows):
        one[r : r + 1, :] = first[:, r * LANES : (r + 1) * LANES]
        two[r : r + 1, :] = second[:, r * LANES : (r + 1) * LANES]
    blank = jnp.zeros((one.shape[0] - rows, LANES), F32)
    one[rows:, :] = blank
    two[rows:, :] = blank


def owner_kernel(rows, parts, first, second, fresh_one, fresh_two, send, grad, one, two, both):
    total = jnp.sum(parts[...].astype(F32), axis=0)
    part = total.shape[0]
    for i in range(total.shape[1] // LANES):
        grad[part * i : part * (i + 1), :] = total[:, i * LANES : (i + 1) * LANES]
    own_moments(rows, first, second, one, two)
    fresh = adam_moments(grad[...], one[...], two[...])
    fresh_one[...], fresh_two[...] = fresh
    for i in range(2):
        for r in range(rows):
            both[i : i + 1, r * LANES : (r + 1) * LANES] = fresh[i][r : r + 1, :]
    packed = both[...].astype(BF16)
    for j in range(send.shape[0]):
        send[j] = packed


def row_kernel(source, out, wide):
    count = source.shape[0]
    for z in range(count):
        pair = source[z].astype(F32)
        for i in range(2):
            wide[i * count + z : i * count + z + 1, :] = pair[i : i + 1]
    values = wide[...].astype(BF16)
    for y in range(out.shape[0]):
        out[y] = values


def written_kernel(rows, me, own_one, own_two, moments, flat, mask, own, out, one, two, fresh, mine, sems):
    count = moments.shape[1] // 2
    steps = sems.shape[0] - 1
    per_step = moments.shape[0] // steps
    tall = per_step * count * rows
    values = own_one[...], own_two[...]
    values = (adam_param(flat[pl.ds(me[0] * rows, own_one.shape[0]), :], *values),) + values
    for i in range(3):
        for r in range(rows):
            mine[i, :, r * LANES : (r + 1) * LANES] = values[i][r : r + 1, :]
    copies = [pltpu.make_async_copy(mine, own, sems.at[steps])]
    copies[0].start()
    for s in range(steps):
        for y in range(s * per_step, (s + 1) * per_step):
            for r in range(rows):
                values = moments[y, :, r * LANES : (r + 1) * LANES].astype(F32)
                at = pl.ds(y * count * rows + r, count, stride=rows)
                one[at, :] = values[:count]
                two[at, :] = values[count:]
        for r in range(s * tall, (s + 1) * tall, 24):
            at = slice(r, r + 24)
            keep = mask[at, :] > 0.0
            fresh_one, fresh_two = one[at, :], two[at, :]
            updated = adam_param(flat[at, :], fresh_one, fresh_two)
            for i, values in enumerate((updated, fresh_one, fresh_two)):
                fresh[i, at, :] = jnp.where(keep, values, 0.0)
        block = pl.ds(s * tall, tall)
        copies.append(pltpu.make_async_copy(fresh.at[:, block], out.at[:, block], sems.at[s]))
        copies[-1].start()
    for copy in copies:
        copy.wait()


def body(dp, activations, cotangent, factor_down, factor_up, first_moment, second_moment, piece_lengths, writers):
    dp_count = lax.axis_size(dp)
    part_len = first_moment.shape[1]
    rows = part_len // LANES
    all_rows = rows * dp_count
    part = 4
    lanes = -(-rows // part) * LANES
    tokens, width = activations.shape
    rank = factor_up.shape[0]
    me = lax.axis_index(dp).astype(jnp.int32).reshape(1)
    down_t = factor_down.T
    x_count = lax.axis_size("x")

    partial, act_copy, cot_copy = pl.pallas_call(
        low_rank_kernel,
        out_shape=(
            jax.ShapeDtypeStruct((tokens, 2 * rank), BF16),
            jax.ShapeDtypeStruct((tokens, width), BF16),
            jax.ShapeDtypeStruct((tokens, width), BF16),
        ),
        in_specs=[HBM] * 4,
        out_specs=(VMEM, VMEM, VMEM),
        scratch_shapes=[
            pltpu.VMEM((rank, width), F32),
            pltpu.VMEM((rank, width), F32),
            pltpu.SemaphoreType.DMA((4,)),
        ],
        compiler_params=PARAMS,
        name="low_rank",
    )(*[pltpu.with_memory_space_constraint(v, pltpu.HBM) for v in (activations, cotangent, down_t, factor_up)])
    other = lax.ppermute(partial, "c", [(0, 1), (1, 0)])
    flat_param, mask = pl.pallas_call(
        param_kernel,
        out_shape=(
            jax.ShapeDtypeStruct((all_rows + 8, LANES), F32),
            jax.ShapeDtypeStruct((all_rows, LANES), F32),
        ),
        in_specs=[SMEM] * 3 + [VMEM] * 2,
        out_specs=(VMEM, VMEM),
        scratch_shapes=[pltpu.VMEM((width, LANES), F32)],
        compiler_params=PARAMS,
        name="flat_param",
    )(me, piece_lengths, writers, down_t, factor_up)
    copies = pl.pallas_call(
        add_copies_kernel,
        out_shape=jax.ShapeDtypeStruct((x_count, tokens, 2 * rank), BF16),
        in_specs=[VMEM, VMEM, pl.BlockSpec(memory_space=pl.ANY)],
        out_specs=VMEM,
        compiler_params=PARAMS,
        name="add_cores",
    )(partial, other, mask)
    parts = lax.all_to_all(copies, "x", 0, 0)
    chunks = pl.pallas_call(
        functools.partial(grad_kernel, rows),
        out_shape=jax.ShapeDtypeStruct((dp_count, part, lanes), BF16),
        in_specs=[VMEM] * 3,
        out_specs=VMEM,
        scratch_shapes=[
            pltpu.VMEM((all_rows + 8, LANES), F32),
            pltpu.VMEM((width, LANES), F32),
        ],
        compiler_params=PARAMS,
        name="grads",
    )(parts, act_copy, cot_copy)
    mine = lax.all_to_all(chunks, dp, 0, 0)
    half = lanes * part // LANES
    z_count = lax.axis_size(dp[1])
    own_one, own_two, send = pl.pallas_call(
        functools.partial(owner_kernel, rows),
        out_shape=(
            jax.ShapeDtypeStruct((half, LANES), F32),
            jax.ShapeDtypeStruct((half, LANES), F32),
            jax.ShapeDtypeStruct((z_count, 2, part_len), BF16),
        ),
        in_specs=[VMEM] * 3,
        out_specs=(VMEM, VMEM, VMEM),
        scratch_shapes=[pltpu.VMEM((half, LANES), F32)] * 3 + [pltpu.VMEM((2, part_len), F32)],
        compiler_params=PARAMS,
        name="owner",
    )(mine, first_moment, second_moment)
    row = lax.all_to_all(send, dp[1], 0, 0)
    row_copies = pl.pallas_call(
        row_kernel,
        out_shape=jax.ShapeDtypeStruct((lax.axis_size(dp[0]), 2 * z_count, part_len), BF16),
        in_specs=[VMEM],
        out_specs=VMEM,
        scratch_shapes=[pltpu.VMEM((2 * z_count, part_len), F32)],
        compiler_params=PARAMS,
        name="row_copies",
    )(row)
    moments = lax.all_to_all(row_copies, dp[0], 0, 0)
    partition, written = pl.pallas_call(
        functools.partial(written_kernel, rows),
        out_shape=(
            jax.ShapeDtypeStruct((3, 1, part_len), F32),
            jax.ShapeDtypeStruct((3, all_rows, LANES), F32),
        ),
        in_specs=[SMEM] + [VMEM] * 5,
        out_specs=(HBM, HBM),
        scratch_shapes=[
            pltpu.VMEM((all_rows, LANES), F32),
            pltpu.VMEM((all_rows, LANES), F32),
            pltpu.VMEM((3, all_rows, LANES), F32),
            pltpu.VMEM((3, 1, part_len), F32),
            pltpu.SemaphoreType.DMA((5,)),
        ],
        compiler_params=PARAMS,
        name="written",
    )(me, own_one, own_two, moments, flat_param, mask)
    return (partition, written.reshape(3, 1, 1, all_rows * LANES))


def solution(mesh):
    fine = Mesh(mesh.devices.reshape(8, 12, 4, 2), ("y", "z", "x", "c"))
    return on_mesh(fine)


def on_mesh(fine):
    dp, tensor = ("y", "z"), ("x", "c")
    in_specs = (
        P(dp, tensor),
        P(dp, tensor),
        P(tensor, None),
        P(None, tensor),
        P(tensor, dp),
        P(tensor, dp),
        P(tensor, None),
        P(tensor, None),
    )
    out_specs = (P(None, tensor, dp), P(None, dp, tensor, None))
    return jax.shard_map(
        functools.partial(body, dp), mesh=fine, in_specs=in_specs, out_specs=out_specs, check_vma=False
    )
```

```python
import functools

import jax
import jax.numpy as jnp
from jax import lax
from jax.experimental import pallas as pl
from jax.experimental.pallas import tpu as pltpu
from jax.sharding import Mesh, PartitionSpec as P

BF16 = jnp.bfloat16
F32 = jnp.float32
LANES = 128
VMEM = pl.BlockSpec(memory_space=pltpu.VMEM)
HBM = pl.BlockSpec(memory_space=pltpu.HBM)
NT = (((1,), (1,)), ((), ()))
PARAMS = pltpu.CompilerParams(vmem_limit_bytes=16 * 1024 * 1024)


def store_flat(flat, wide, down_t2, up):
    width = up.shape[1]
    rank = up.shape[0]
    half = width // 2
    per_row = width // LANES
    wide[...] = down_t2.T
    even = wide[pl.ds(0, half, stride=2), :]
    odd = wide[pl.ds(1, half, stride=2), :]
    lane = lax.broadcasted_iota(jnp.int32, (half, LANES), 1)
    flat[0:half, :] = jnp.where(lane < rank, even, odd)
    for c in range(per_row):
        flat[pl.ds(half + c, rank, stride=per_row), :] = up[:, c * LANES : (c + 1) * LANES]
    used = half + rank * per_row
    flat[used:, :] = jnp.zeros((flat.shape[0] - used, LANES), F32)


def mark_pieces(dp, lengths, writers, mask):
    me = lax.axis_index(dp)
    mask[...] = jnp.zeros_like(mask)
    block = 8 * LANES
    spot = lax.broadcasted_iota(jnp.int32, (8, LANES), 0) * LANES + lax.broadcasted_iota(
        jnp.int32, (8, LANES), 1
    )

    def piece(k, start):
        end = start + lengths[0, k]

        @pl.when(writers[0, k] == me)
        def _():
            def mark(b, carry):
                here = spot + b * block
                at = pl.ds(pl.multiple_of(b * 8, 8), 8)
                inside = jnp.logical_and(here >= start, here < end)
                mask[at, :] = jnp.where(inside, 1.0, mask[at, :])
                return carry

            lax.fori_loop(start // block, (end + block - 1) // block, mark, 0)

        return end

    group = 8
    begin = jnp.int32(0)
    for low in range(0, lengths.shape[1], group):
        hit = writers[0, low] == me
        total = lengths[0, low]
        for k in range(low + 1, low + group):
            hit = jnp.logical_or(hit, writers[0, k] == me)
            total += lengths[0, k]

        @pl.when(hit)
        def _(low=low, begin=begin):
            lax.fori_loop(low, low + group, piece, begin)

        begin += total


def low_rank_kernel(
    dp, act, cot, down_t, up, lengths, writers, out, a, c, flat, mask, d, u, wide, long, who, sems
):
    pairs = ((down_t, d), (up, u), (act, a), (cot, c), (lengths, long), (writers, who))
    copies = [pltpu.make_async_copy(source, target, sems.at[i]) for i, (source, target) in enumerate(pairs)]
    for copy in copies:
        copy.start()
    copies[0].wait()
    copies[1].wait()
    left, right = d[...], u[...]
    store_flat(flat, wide, jnp.concatenate([left, left], axis=0), right)
    down_b, up_b = left.astype(BF16), right.astype(BF16)
    blank = jnp.zeros_like(down_b)
    copies[4].wait()
    copies[5].wait()
    mark_pieces(dp, long, who, mask)
    copies[2].wait()
    both = lax.dot_general(a[...], jnp.concatenate([down_b, blank], axis=0), NT, preferred_element_type=F32)
    copies[3].wait()
    both += lax.dot_general(c[...], jnp.concatenate([blank, up_b], axis=0), NT, preferred_element_type=F32)
    out[...] = both.astype(BF16)


def add_copies_kernel(mine, other, out):
    total = (mine[...].astype(F32) + other[...].astype(F32)).astype(BF16)
    for i in range(out.shape[0]):
        out[i] = total


def grad_kernel(rows, parts, act, cot, out, flat, wide):
    total = parts[0].astype(F32)
    for i in range(1, parts.shape[0]):
        total += parts[i].astype(F32)
    turned = total.T.astype(BF16)
    rank = turned.shape[0] // 2
    projected = turned[rank:]
    twice = jnp.concatenate([projected, projected], axis=0)
    up = 2.0 * jnp.dot(turned[:rank], cot[...], preferred_element_type=F32)
    down = 2.0 * jnp.dot(twice, act[...], preferred_element_type=F32)
    store_flat(flat, wide, down, up)
    part = out.shape[1]
    for j in range(out.shape[0]):
        for i in range(out.shape[2] // LANES):
            at = rows * j + part * i
            out[j, :, i * LANES : (i + 1) * LANES] = flat[at : at + part, :].astype(BF16)


def adam_moments(grad, moment_one, moment_two):
    return 0.9 * moment_one + 0.1 * grad, 0.999 * moment_two + 0.001 * grad * grad


def adam_param(param, fresh_one, fresh_two):
    fixed_one = 1.0 - 0.9**10
    fixed_two = 1.0 - 0.999**10
    return param - 0.01 * (fresh_one / fixed_one) / (jnp.sqrt(fresh_two / fixed_two) + 1e-08)


def own_moments(rows, first, second, one, two):
    for r in range(rows):
        one[r : r + 1, :] = first[:, r * LANES : (r + 1) * LANES]
        two[r : r + 1, :] = second[:, r * LANES : (r + 1) * LANES]
    blank = jnp.zeros((one.shape[0] - rows, LANES), F32)
    one[rows:, :] = blank
    two[rows:, :] = blank


def owner_kernel(rows, parts, first, second, fresh_one, fresh_two, send, grad, one, two, both):
    total = jnp.sum(parts[...].astype(F32), axis=0)
    part = total.shape[0]
    for i in range(total.shape[1] // LANES):
        grad[part * i : part * (i + 1), :] = total[:, i * LANES : (i + 1) * LANES]
    own_moments(rows, first, second, one, two)
    fresh = adam_moments(grad[...], one[...], two[...])
    fresh_one[...], fresh_two[...] = fresh
    for i in range(2):
        for r in range(rows):
            both[i : i + 1, r * LANES : (r + 1) * LANES] = fresh[i][r : r + 1, :]
    packed = both[...].astype(BF16)
    for j in range(send.shape[0]):
        send[j] = packed


def row_kernel(source, out, wide):
    count = source.shape[0]
    for z in range(count):
        pair = source[z].astype(F32)
        for i in range(2):
            wide[i * count + z : i * count + z + 1, :] = pair[i : i + 1]
    values = wide[...].astype(BF16)
    for y in range(out.shape[0]):
        out[y] = values


def written_kernel(rows, dp, own_one, own_two, moments, flat, mask, own, out, one, two, fresh, mine, sems):
    count = moments.shape[1] // 2
    steps = sems.shape[0] - 1
    per_step = moments.shape[0] // steps
    tall = per_step * count * rows
    values = own_one[...], own_two[...]
    values = (adam_param(flat[pl.ds(lax.axis_index(dp) * rows, own_one.shape[0]), :], *values),) + values
    for i in range(3):
        for r in range(rows):
            mine[i, :, r * LANES : (r + 1) * LANES] = values[i][r : r + 1, :]
    copies = [pltpu.make_async_copy(mine, own, sems.at[steps])]
    copies[0].start()
    for s in range(steps):
        for y in range(s * per_step, (s + 1) * per_step):
            for r in range(rows):
                values = moments[y, :, r * LANES : (r + 1) * LANES].astype(F32)
                at = pl.ds(y * count * rows + r, count, stride=rows)
                one[at, :] = values[:count]
                two[at, :] = values[count:]
        for r in range(s * tall, (s + 1) * tall, 24):
            at = slice(r, r + 24)
            keep = mask[at, :] > 0.0
            fresh_one, fresh_two = one[at, :], two[at, :]
            updated = adam_param(flat[at, :], fresh_one, fresh_two)
            for i, values in enumerate((updated, fresh_one, fresh_two)):
                fresh[i, at, :] = jnp.where(keep, values, 0.0)
        block = pl.ds(s * tall, tall)
        copies.append(pltpu.make_async_copy(fresh.at[:, block], out.at[:, block], sems.at[s]))
        copies[-1].start()
    for copy in copies:
        copy.wait()


def body(dp, activations, cotangent, factor_down, factor_up, first_moment, second_moment, piece_lengths, writers):
    dp_count = lax.axis_size(dp)
    part_len = first_moment.shape[1]
    rows = part_len // LANES
    all_rows = rows * dp_count
    part = 4
    lanes = -(-rows // part) * LANES
    tokens, width = activations.shape
    rank = factor_up.shape[0]
    down_t = factor_down.T
    x_count = lax.axis_size("x")

    first_in = (activations, cotangent, down_t, factor_up, piece_lengths, writers)
    partial, act_copy, cot_copy, flat_param, mask = pl.pallas_call(
        functools.partial(low_rank_kernel, dp),
        out_shape=(
            jax.ShapeDtypeStruct((tokens, 2 * rank), BF16),
            jax.ShapeDtypeStruct((tokens, width), BF16),
            jax.ShapeDtypeStruct((tokens, width), BF16),
            jax.ShapeDtypeStruct((all_rows + 8, LANES), F32),
            jax.ShapeDtypeStruct((all_rows, LANES), F32),
        ),
        in_specs=[HBM] * 6,
        out_specs=[VMEM] * 5,
        scratch_shapes=[
            pltpu.VMEM((rank, width), F32),
            pltpu.VMEM((rank, width), F32),
            pltpu.VMEM((width, LANES), F32),
            pltpu.SMEM(piece_lengths.shape, jnp.int32),
            pltpu.SMEM(writers.shape, jnp.int32),
            pltpu.SemaphoreType.DMA((6,)),
        ],
        compiler_params=PARAMS,
        name="low_rank",
    )(*[pltpu.with_memory_space_constraint(v, pltpu.HBM) for v in first_in])
    other = lax.ppermute(partial, "c", [(0, 1), (1, 0)])
    copies = pl.pallas_call(
        add_copies_kernel,
        out_shape=jax.ShapeDtypeStruct((x_count, tokens, 2 * rank), BF16),
        in_specs=[VMEM] * 2,
        out_specs=VMEM,
        compiler_params=PARAMS,
        name="add_cores",
    )(partial, other)
    parts = lax.all_to_all(copies, "x", 0, 0)
    chunks = pl.pallas_call(
        functools.partial(grad_kernel, rows),
        out_shape=jax.ShapeDtypeStruct((dp_count, part, lanes), BF16),
        in_specs=[VMEM] * 3,
        out_specs=VMEM,
        scratch_shapes=[
            pltpu.VMEM((all_rows + 8, LANES), F32),
            pltpu.VMEM((width, LANES), F32),
        ],
        compiler_params=PARAMS,
        name="grads",
    )(parts, act_copy, cot_copy)
    mine = lax.all_to_all(chunks, dp, 0, 0)
    half = lanes * part // LANES
    z_count = lax.axis_size(dp[1])
    own_one, own_two, send = pl.pallas_call(
        functools.partial(owner_kernel, rows),
        out_shape=(
            jax.ShapeDtypeStruct((half, LANES), F32),
            jax.ShapeDtypeStruct((half, LANES), F32),
            jax.ShapeDtypeStruct((z_count, 2, part_len), BF16),
        ),
        in_specs=[VMEM] * 3,
        out_specs=(VMEM, VMEM, VMEM),
        scratch_shapes=[pltpu.VMEM((half, LANES), F32)] * 3 + [pltpu.VMEM((2, part_len), F32)],
        compiler_params=PARAMS,
        name="owner",
    )(mine, first_moment, second_moment)
    row = lax.all_to_all(send, dp[1], 0, 0)
    row_copies = pl.pallas_call(
        row_kernel,
        out_shape=jax.ShapeDtypeStruct((lax.axis_size(dp[0]), 2 * z_count, part_len), BF16),
        in_specs=[VMEM],
        out_specs=VMEM,
        scratch_shapes=[pltpu.VMEM((2 * z_count, part_len), F32)],
        compiler_params=PARAMS,
        name="row_copies",
    )(row)
    moments = lax.all_to_all(row_copies, dp[0], 0, 0)
    partition, written = pl.pallas_call(
        functools.partial(written_kernel, rows, dp),
        out_shape=(
            jax.ShapeDtypeStruct((3, 1, part_len), F32),
            jax.ShapeDtypeStruct((3, all_rows, LANES), F32),
        ),
        in_specs=[VMEM] * 5,
        out_specs=(HBM, HBM),
        scratch_shapes=[
            pltpu.VMEM((all_rows, LANES), F32),
            pltpu.VMEM((all_rows, LANES), F32),
            pltpu.VMEM((3, all_rows, LANES), F32),
            pltpu.VMEM((3, 1, part_len), F32),
            pltpu.SemaphoreType.DMA((5,)),
        ],
        compiler_params=PARAMS,
        name="written",
    )(own_one, own_two, moments, flat_param, mask)
    return (partition, written.reshape(3, 1, 1, all_rows * LANES))


def solution(mesh):
    fine = Mesh(mesh.devices.reshape(8, 12, 4, 2), ("y", "z", "x", "c"))
    return on_mesh(fine)


def on_mesh(fine):
    dp, tensor = ("y", "z"), ("x", "c")
    in_specs = (
        P(dp, tensor),
        P(dp, tensor),
        P(tensor, None),
        P(None, tensor),
        P(tensor, dp),
        P(tensor, dp),
        P(tensor, None),
        P(tensor, None),
    )
    out_specs = (P(None, tensor, dp), P(None, dp, tensor, None))
    return jax.shard_map(
        functools.partial(body, dp), mesh=fine, in_specs=in_specs, out_specs=out_specs, check_vma=False
    )
```

```python
import functools

import jax
import jax.numpy as jnp
from jax import lax
from jax.experimental import pallas as pl
from jax.experimental.pallas import tpu as pltpu
from jax.sharding import Mesh, PartitionSpec as P

BF16 = jnp.bfloat16
F32 = jnp.float32
LANES = 128
VMEM = pl.BlockSpec(memory_space=pltpu.VMEM)
HBM = pl.BlockSpec(memory_space=pltpu.HBM)
NT = (((1,), (1,)), ((), ()))
PARAMS = pltpu.CompilerParams(vmem_limit_bytes=16 * 1024 * 1024)


def store_flat(flat, wide, down_t2, up):
    width = up.shape[1]
    rank = up.shape[0]
    half = width // 2
    per_row = width // LANES
    wide[...] = down_t2.T
    even = wide[pl.ds(0, half, stride=2), :]
    odd = wide[pl.ds(1, half, stride=2), :]
    lane = lax.broadcasted_iota(jnp.int32, (half, LANES), 1)
    flat[0:half, :] = jnp.where(lane < rank, even, odd)
    for c in range(per_row):
        flat[pl.ds(half + c, rank, stride=per_row), :] = up[:, c * LANES : (c + 1) * LANES]
    used = half + rank * per_row
    flat[used:, :] = jnp.zeros((flat.shape[0] - used, LANES), F32)


def mark_pieces(dp, lengths, writers, mask):
    me = lax.axis_index(dp)
    mask[...] = jnp.zeros_like(mask)
    block = 8 * LANES
    spot = lax.broadcasted_iota(jnp.int32, (8, LANES), 0) * LANES + lax.broadcasted_iota(
        jnp.int32, (8, LANES), 1
    )

    def piece(k, start):
        end = start + lengths[0, k]

        @pl.when(writers[0, k] == me)
        def _():
            def mark(b, carry):
                here = spot + b * block
                at = pl.ds(pl.multiple_of(b * 8, 8), 8)
                inside = jnp.logical_and(here >= start, here < end)
                mask[at, :] = jnp.where(inside, 1.0, mask[at, :])
                return carry

            lax.fori_loop(start // block, (end + block - 1) // block, mark, 0)

        return end

    group = 8
    begin = jnp.int32(0)
    for low in range(0, lengths.shape[1], group):
        hit = writers[0, low] == me
        total = lengths[0, low]
        for k in range(low + 1, low + group):
            hit = jnp.logical_or(hit, writers[0, k] == me)
            total += lengths[0, k]

        @pl.when(hit)
        def _(low=low, begin=begin):
            lax.fori_loop(low, low + group, piece, begin)

        begin += total


def low_rank_kernel(
    dp, act, cot, down_t, up, lengths, writers, out, a, c, flat, mask, d, u, wide, long, who, sems
):
    pairs = ((down_t, d), (up, u), (act, a), (cot, c), (lengths, long), (writers, who))
    copies = [pltpu.make_async_copy(source, target, sems.at[i]) for i, (source, target) in enumerate(pairs)]
    for copy in copies:
        copy.start()
    copies[0].wait()
    copies[1].wait()
    left, right = d[...], u[...]
    store_flat(flat, wide, jnp.concatenate([left, left], axis=0), right)
    down_b, up_b = left.astype(BF16), right.astype(BF16)
    blank = jnp.zeros_like(down_b)
    copies[4].wait()
    copies[5].wait()
    mark_pieces(dp, long, who, mask)
    copies[2].wait()
    both = lax.dot_general(a[...], jnp.concatenate([down_b, blank], axis=0), NT, preferred_element_type=F32)
    copies[3].wait()
    both += lax.dot_general(c[...], jnp.concatenate([blank, up_b], axis=0), NT, preferred_element_type=F32)
    out[...] = both.astype(BF16)


def add_copies_kernel(mine, other, out):
    total = (mine[...].astype(F32) + other[...].astype(F32)).astype(BF16)
    for i in range(out.shape[0]):
        out[i] = total


def grad_kernel(rows, parts, act, cot, out, flat, wide):
    total = parts[0].astype(F32)
    for i in range(1, parts.shape[0]):
        total += parts[i].astype(F32)
    turned = total.T.astype(BF16)
    rank = turned.shape[0] // 2
    projected = turned[rank:]
    twice = jnp.concatenate([projected, projected], axis=0)
    up = 2.0 * jnp.dot(turned[:rank], cot[...], preferred_element_type=F32)
    down = 2.0 * jnp.dot(twice, act[...], preferred_element_type=F32)
    store_flat(flat, wide, down, up)
    for j in range(out.shape[0]):
        out[j] = flat[rows * j : rows * j + out.shape[1], :].astype(BF16)


def slab_kernel(rows, parts, out, slab):
    total = parts[0].astype(F32)
    for j in range(1, parts.shape[0]):
        total += parts[j].astype(F32)
    slab[...] = total
    part = out.shape[1]
    for j in range(out.shape[0]):
        for i in range(out.shape[2] // LANES):
            at = rows * j + part * i
            out[j, :, i * LANES : (i + 1) * LANES] = slab[at : at + part, :].astype(BF16)


def adam_moments(grad, moment_one, moment_two):
    return 0.9 * moment_one + 0.1 * grad, 0.999 * moment_two + 0.001 * grad * grad


def adam_param(param, fresh_one, fresh_two):
    fixed_one = 1.0 - 0.9**10
    fixed_two = 1.0 - 0.999**10
    return param - 0.01 * (fresh_one / fixed_one) / (jnp.sqrt(fresh_two / fixed_two) + 1e-08)


def own_moments(rows, first, second, one, two):
    for r in range(rows):
        one[r : r + 1, :] = first[:, r * LANES : (r + 1) * LANES]
        two[r : r + 1, :] = second[:, r * LANES : (r + 1) * LANES]
    blank = jnp.zeros((one.shape[0] - rows, LANES), F32)
    one[rows:, :] = blank
    two[rows:, :] = blank


def owner_kernel(rows, parts, first, second, fresh_one, fresh_two, send, grad, one, two, both):
    total = jnp.sum(parts[...].astype(F32), axis=0)
    part = total.shape[0]
    for i in range(total.shape[1] // LANES):
        grad[part * i : part * (i + 1), :] = total[:, i * LANES : (i + 1) * LANES]
    own_moments(rows, first, second, one, two)
    fresh = adam_moments(grad[...], one[...], two[...])
    fresh_one[...], fresh_two[...] = fresh
    for i in range(2):
        for r in range(rows):
            both[i : i + 1, r * LANES : (r + 1) * LANES] = fresh[i][r : r + 1, :]
    packed = both[...].astype(BF16)
    for j in range(send.shape[0]):
        send[j] = packed


def row_kernel(source, out, wide):
    count = source.shape[0]
    for z in range(count):
        pair = source[z].astype(F32)
        for i in range(2):
            wide[i * count + z : i * count + z + 1, :] = pair[i : i + 1]
    values = wide[...].astype(BF16)
    for y in range(out.shape[0]):
        out[y] = values


def written_kernel(rows, dp, own_one, own_two, moments, flat, mask, own, out, one, two, fresh, mine, sems):
    count = moments.shape[1] // 2
    steps = sems.shape[0] - 1
    per_step = moments.shape[0] // steps
    tall = per_step * count * rows
    values = own_one[...], own_two[...]
    values = (adam_param(flat[pl.ds(lax.axis_index(dp) * rows, own_one.shape[0]), :], *values),) + values
    for i in range(3):
        for r in range(rows):
            mine[i, :, r * LANES : (r + 1) * LANES] = values[i][r : r + 1, :]
    copies = [pltpu.make_async_copy(mine, own, sems.at[steps])]
    copies[0].start()
    for s in range(steps):
        for y in range(s * per_step, (s + 1) * per_step):
            for r in range(rows):
                values = moments[y, :, r * LANES : (r + 1) * LANES].astype(F32)
                at = pl.ds(y * count * rows + r, count, stride=rows)
                one[at, :] = values[:count]
                two[at, :] = values[count:]
        for r in range(s * tall, (s + 1) * tall, 24):
            at = slice(r, r + 24)
            keep = mask[at, :] > 0.0
            fresh_one, fresh_two = one[at, :], two[at, :]
            updated = adam_param(flat[at, :], fresh_one, fresh_two)
            for i, values in enumerate((updated, fresh_one, fresh_two)):
                fresh[i, at, :] = jnp.where(keep, values, 0.0)
        block = pl.ds(s * tall, tall)
        copies.append(pltpu.make_async_copy(fresh.at[:, block], out.at[:, block], sems.at[s]))
        copies[-1].start()
    for copy in copies:
        copy.wait()


def body(dp, activations, cotangent, factor_down, factor_up, first_moment, second_moment, piece_lengths, writers):
    dp_count = lax.axis_size(dp)
    part_len = first_moment.shape[1]
    rows = part_len // LANES
    all_rows = rows * dp_count
    part = 4
    lanes = -(-rows // part) * LANES
    tokens, width = activations.shape
    rank = factor_up.shape[0]
    down_t = factor_down.T
    x_count = lax.axis_size("x")

    first_in = (activations, cotangent, down_t, factor_up, piece_lengths, writers)
    partial, act_copy, cot_copy, flat_param, mask = pl.pallas_call(
        functools.partial(low_rank_kernel, dp),
        out_shape=(
            jax.ShapeDtypeStruct((tokens, 2 * rank), BF16),
            jax.ShapeDtypeStruct((tokens, width), BF16),
            jax.ShapeDtypeStruct((tokens, width), BF16),
            jax.ShapeDtypeStruct((all_rows + 8, LANES), F32),
            jax.ShapeDtypeStruct((all_rows, LANES), F32),
        ),
        in_specs=[HBM] * 6,
        out_specs=[VMEM] * 5,
        scratch_shapes=[
            pltpu.VMEM((rank, width), F32),
            pltpu.VMEM((rank, width), F32),
            pltpu.VMEM((width, LANES), F32),
            pltpu.SMEM(piece_lengths.shape, jnp.int32),
            pltpu.SMEM(writers.shape, jnp.int32),
            pltpu.SemaphoreType.DMA((6,)),
        ],
        compiler_params=PARAMS,
        name="low_rank",
    )(*[pltpu.with_memory_space_constraint(v, pltpu.HBM) for v in first_in])
    other = lax.ppermute(partial, "c", [(0, 1), (1, 0)])
    copies = pl.pallas_call(
        add_copies_kernel,
        out_shape=jax.ShapeDtypeStruct((x_count, tokens, 2 * rank), BF16),
        in_specs=[VMEM] * 2,
        out_specs=VMEM,
        compiler_params=PARAMS,
        name="add_cores",
    )(partial, other)
    parts = lax.all_to_all(copies, "x", 0, 0)
    y_count, z_count = lax.axis_size(dp[0]), lax.axis_size(dp[1])
    slab = rows * z_count
    tall = -(-slab // 8) * 8
    slabs = pl.pallas_call(
        functools.partial(grad_kernel, slab),
        out_shape=jax.ShapeDtypeStruct((y_count, tall, LANES), BF16),
        in_specs=[VMEM] * 3,
        out_specs=VMEM,
        scratch_shapes=[
            pltpu.VMEM((all_rows + 8, LANES), F32),
            pltpu.VMEM((width, LANES), F32),
        ],
        compiler_params=PARAMS,
        name="grads",
    )(parts, act_copy, cot_copy)
    column = lax.all_to_all(slabs, dp[0], 0, 0)
    chunks = pl.pallas_call(
        functools.partial(slab_kernel, rows),
        out_shape=jax.ShapeDtypeStruct((z_count, part, lanes), BF16),
        in_specs=[VMEM],
        out_specs=VMEM,
        scratch_shapes=[pltpu.VMEM((tall, LANES), F32)],
        compiler_params=PARAMS,
        name="slab",
    )(column)
    mine = lax.all_to_all(chunks, dp[1], 0, 0)
    half = lanes * part // LANES
    own_one, own_two, send = pl.pallas_call(
        functools.partial(owner_kernel, rows),
        out_shape=(
            jax.ShapeDtypeStruct((half, LANES), F32),
            jax.ShapeDtypeStruct((half, LANES), F32),
            jax.ShapeDtypeStruct((z_count, 2, part_len), BF16),
        ),
        in_specs=[VMEM] * 3,
        out_specs=(VMEM, VMEM, VMEM),
        scratch_shapes=[pltpu.VMEM((half, LANES), F32)] * 3 + [pltpu.VMEM((2, part_len), F32)],
        compiler_params=PARAMS,
        name="owner",
    )(mine, first_moment, second_moment)
    row = lax.all_to_all(send, dp[1], 0, 0)
    row_copies = pl.pallas_call(
        row_kernel,
        out_shape=jax.ShapeDtypeStruct((lax.axis_size(dp[0]), 2 * z_count, part_len), BF16),
        in_specs=[VMEM],
        out_specs=VMEM,
        scratch_shapes=[pltpu.VMEM((2 * z_count, part_len), F32)],
        compiler_params=PARAMS,
        name="row_copies",
    )(row)
    moments = lax.all_to_all(row_copies, dp[0], 0, 0)
    partition, written = pl.pallas_call(
        functools.partial(written_kernel, rows, dp),
        out_shape=(
            jax.ShapeDtypeStruct((3, 1, part_len), F32),
            jax.ShapeDtypeStruct((3, all_rows, LANES), F32),
        ),
        in_specs=[VMEM] * 5,
        out_specs=(HBM, HBM),
        scratch_shapes=[
            pltpu.VMEM((all_rows, LANES), F32),
            pltpu.VMEM((all_rows, LANES), F32),
            pltpu.VMEM((3, all_rows, LANES), F32),
            pltpu.VMEM((3, 1, part_len), F32),
            pltpu.SemaphoreType.DMA((5,)),
        ],
        compiler_params=PARAMS,
        name="written",
    )(own_one, own_two, moments, flat_param, mask)
    return (partition, written.reshape(3, 1, 1, all_rows * LANES))


def solution(mesh):
    fine = Mesh(mesh.devices.reshape(8, 12, 4, 2), ("y", "z", "x", "c"))
    return on_mesh(fine)


def on_mesh(fine):
    dp, tensor = ("y", "z"), ("x", "c")
    in_specs = (
        P(dp, tensor),
        P(dp, tensor),
        P(tensor, None),
        P(None, tensor),
        P(tensor, dp),
        P(tensor, dp),
        P(tensor, None),
        P(tensor, None),
    )
    out_specs = (P(None, tensor, dp), P(None, dp, tensor, None))
    return jax.shard_map(
        functools.partial(body, dp), mesh=fine, in_specs=in_specs, out_specs=out_specs, check_vma=False
    )
```

```python
import functools

import jax
import jax.numpy as jnp
from jax import lax
from jax.experimental import pallas as pl
from jax.experimental.pallas import tpu as pltpu
from jax.sharding import Mesh, PartitionSpec as P

BF16 = jnp.bfloat16
F32 = jnp.float32
LANES = 128
VMEM = pl.BlockSpec(memory_space=pltpu.VMEM)
HBM = pl.BlockSpec(memory_space=pltpu.HBM)
NT = (((1,), (1,)), ((), ()))
PARAMS = pltpu.CompilerParams(vmem_limit_bytes=16 * 1024 * 1024)


def store_flat(flat, wide, down_t2, up):
    width = up.shape[1]
    rank = up.shape[0]
    half = width // 2
    per_row = width // LANES
    wide[...] = down_t2.T
    even = wide[pl.ds(0, half, stride=2), :]
    odd = wide[pl.ds(1, half, stride=2), :]
    lane = lax.broadcasted_iota(jnp.int32, (half, LANES), 1)
    flat[0:half, :] = jnp.where(lane < rank, even, odd)
    for c in range(per_row):
        flat[pl.ds(half + c, rank, stride=per_row), :] = up[:, c * LANES : (c + 1) * LANES]
    used = half + rank * per_row
    flat[used:, :] = jnp.zeros((flat.shape[0] - used, LANES), F32)


def mark_pieces(dp, lengths, writers, mask):
    me = lax.axis_index(dp)
    mask[...] = jnp.zeros_like(mask)
    block = 8 * LANES
    spot = lax.broadcasted_iota(jnp.int32, (8, LANES), 0) * LANES + lax.broadcasted_iota(
        jnp.int32, (8, LANES), 1
    )

    def piece(k, start):
        end = start + lengths[0, k]

        @pl.when(writers[0, k] == me)
        def _():
            def mark(b, carry):
                here = spot + b * block
                at = pl.ds(pl.multiple_of(b * 8, 8), 8)
                inside = jnp.logical_and(here >= start, here < end)
                mask[at, :] = jnp.where(inside, 1.0, mask[at, :])
                return carry

            lax.fori_loop(start // block, (end + block - 1) // block, mark, 0)

        return end

    group = 8
    begin = jnp.int32(0)
    for low in range(0, lengths.shape[1], group):
        hit = writers[0, low] == me
        total = lengths[0, low]
        for k in range(low + 1, low + group):
            hit = jnp.logical_or(hit, writers[0, k] == me)
            total += lengths[0, k]

        @pl.when(hit)
        def _(low=low, begin=begin):
            lax.fori_loop(low, low + group, piece, begin)

        begin += total


def low_rank_kernel(
    dp, act, cot, down_t, up, lengths, writers, out, a, c, flat, mask, d, u, wide, long, who, sems
):
    pairs = ((down_t, d), (up, u), (act, a), (cot, c), (lengths, long), (writers, who))
    copies = [pltpu.make_async_copy(source, target, sems.at[i]) for i, (source, target) in enumerate(pairs)]
    for copy in copies:
        copy.start()
    copies[0].wait()
    copies[1].wait()
    left, right = d[...], u[...]
    store_flat(flat, wide, jnp.concatenate([left, left], axis=0), right)
    down_b, up_b = left.astype(BF16), right.astype(BF16)
    blank = jnp.zeros_like(down_b)
    copies[4].wait()
    copies[5].wait()
    mark_pieces(dp, long, who, mask)
    copies[2].wait()
    both = lax.dot_general(a[...], jnp.concatenate([down_b, blank], axis=0), NT, preferred_element_type=F32)
    copies[3].wait()
    both += lax.dot_general(c[...], jnp.concatenate([blank, up_b], axis=0), NT, preferred_element_type=F32)
    out[...] = both.astype(BF16)


def add_copies_kernel(mine, other, out):
    total = (mine[...].astype(F32) + other[...].astype(F32)).astype(BF16)
    for i in range(out.shape[0]):
        out[i] = total


def grad_kernel(rows, parts, act, cot, out, flat, wide):
    total = parts[0].astype(F32)
    for i in range(1, parts.shape[0]):
        total += parts[i].astype(F32)
    turned = total.T.astype(BF16)
    rank = turned.shape[0] // 2
    projected = turned[rank:]
    twice = jnp.concatenate([projected, projected], axis=0)
    up = 2.0 * jnp.dot(turned[:rank], cot[...], preferred_element_type=F32)
    down = 2.0 * jnp.dot(twice, act[...], preferred_element_type=F32)
    store_flat(flat, wide, down, up)
    for j in range(out.shape[0]):
        out[j] = flat[rows * j : rows * j + out.shape[1], :].astype(BF16)


def store_rows(target, start, source, rows):
    for r in range(rows):
        target[start + r : start + r + 1, :] = source[:, r * LANES : (r + 1) * LANES]


def slab_kernel(rows, parts, first, second, out, both):
    tall = parts.shape[1]
    half = (out.shape[1] - tall) // 2
    total = parts[0].astype(F32)
    for j in range(1, parts.shape[0]):
        total += parts[j].astype(F32)
    both[:tall, :] = total
    both[tall:, :] = jnp.zeros((2 * half, LANES), F32)
    store_rows(both, tall, first, rows)
    store_rows(both, tall + half, second, rows)
    values = both[...].astype(BF16)
    for j in range(out.shape[0]):
        out[j] = values


def adam_moments(grad, moment_one, moment_two):
    return 0.9 * moment_one + 0.1 * grad, 0.999 * moment_two + 0.001 * grad * grad


def adam_param(param, fresh_one, fresh_two):
    fixed_one = 1.0 - 0.9**10
    fixed_two = 1.0 - 0.999**10
    return param - 0.01 * (fresh_one / fixed_one) / (jnp.sqrt(fresh_two / fixed_two) + 1e-08)


def owner_kernel(rows, axis, parts, first, second, own_one, own_two, send, grad, one, two, mine_one, mine_two, both):
    tall = grad.shape[0]
    half = (parts.shape[1] - tall) // 2
    slab = rows * parts.shape[0]
    total = jnp.zeros((tall, LANES), F32)
    for j in range(parts.shape[0]):
        values = parts[j].astype(F32)
        total += values[:tall]
        one[rows * j : rows * j + half, :] = values[tall : tall + half]
        two[rows * j : rows * j + half, :] = values[tall + half :]
    grad[...] = total
    fresh = adam_moments(total[:slab], one[:slab, :], two[:slab, :])
    for i in range(2):
        both[slab * i : slab * (i + 1), :] = fresh[i]
    packed = both[...].astype(BF16)
    for j in range(send.shape[0]):
        send[j] = packed
    blank = jnp.zeros((half - rows, LANES), F32)
    for target, source in ((mine_one, first), (mine_two, second)):
        store_rows(target, 0, source, rows)
        target[rows:, :] = blank
    mine = grad[pl.ds(lax.axis_index(axis) * rows, half), :]
    own_one[...], own_two[...] = adam_moments(mine, mine_one[...], mine_two[...])


def written_kernel(rows, dp, own_one, own_two, moments, flat, mask, own, out, one, two, fresh, mine, sems):
    slab = moments.shape[1] // 2
    steps = sems.shape[0] - 1
    per_step = moments.shape[0] // steps
    tall = per_step * slab
    values = own_one[...], own_two[...]
    values = (adam_param(flat[pl.ds(lax.axis_index(dp) * rows, own_one.shape[0]), :], *values),) + values
    for i in range(3):
        for r in range(rows):
            mine[i, :, r * LANES : (r + 1) * LANES] = values[i][r : r + 1, :]
    copies = [pltpu.make_async_copy(mine, own, sems.at[steps])]
    copies[0].start()
    for s in range(steps):
        for y in range(s * per_step, (s + 1) * per_step):
            values = moments[y].astype(F32)
            one[slab * y : slab * (y + 1), :] = values[:slab]
            two[slab * y : slab * (y + 1), :] = values[slab:]
        for r in range(s * tall, (s + 1) * tall, 24):
            at = slice(r, r + 24)
            keep = mask[at, :] > 0.0
            fresh_one, fresh_two = one[at, :], two[at, :]
            updated = adam_param(flat[at, :], fresh_one, fresh_two)
            for i, values in enumerate((updated, fresh_one, fresh_two)):
                fresh[i, at, :] = jnp.where(keep, values, 0.0)
        block = pl.ds(s * tall, tall)
        copies.append(pltpu.make_async_copy(fresh.at[:, block], out.at[:, block], sems.at[s]))
        copies[-1].start()
    for copy in copies:
        copy.wait()


def body(dp, activations, cotangent, factor_down, factor_up, first_moment, second_moment, piece_lengths, writers):
    dp_count = lax.axis_size(dp)
    part_len = first_moment.shape[1]
    rows = part_len // LANES
    all_rows = rows * dp_count
    tokens, width = activations.shape
    rank = factor_up.shape[0]
    down_t = factor_down.T
    x_count = lax.axis_size("x")

    first_in = (activations, cotangent, down_t, factor_up, piece_lengths, writers)
    partial, act_copy, cot_copy, flat_param, mask = pl.pallas_call(
        functools.partial(low_rank_kernel, dp),
        out_shape=(
            jax.ShapeDtypeStruct((tokens, 2 * rank), BF16),
            jax.ShapeDtypeStruct((tokens, width), BF16),
            jax.ShapeDtypeStruct((tokens, width), BF16),
            jax.ShapeDtypeStruct((all_rows + 8, LANES), F32),
            jax.ShapeDtypeStruct((all_rows, LANES), F32),
        ),
        in_specs=[HBM] * 6,
        out_specs=[VMEM] * 5,
        scratch_shapes=[
            pltpu.VMEM((rank, width), F32),
            pltpu.VMEM((rank, width), F32),
            pltpu.VMEM((width, LANES), F32),
            pltpu.SMEM(piece_lengths.shape, jnp.int32),
            pltpu.SMEM(writers.shape, jnp.int32),
            pltpu.SemaphoreType.DMA((6,)),
        ],
        compiler_params=PARAMS,
        name="low_rank",
    )(*[pltpu.with_memory_space_constraint(v, pltpu.HBM) for v in first_in])
    other = lax.ppermute(partial, "c", [(0, 1), (1, 0)])
    copies = pl.pallas_call(
        add_copies_kernel,
        out_shape=jax.ShapeDtypeStruct((x_count, tokens, 2 * rank), BF16),
        in_specs=[VMEM] * 2,
        out_specs=VMEM,
        compiler_params=PARAMS,
        name="add_cores",
    )(partial, other)
    parts = lax.all_to_all(copies, "x", 0, 0)
    y_count, z_count = lax.axis_size(dp[0]), lax.axis_size(dp[1])
    slab = rows * z_count
    tall = -(-slab // 8) * 8
    slabs = pl.pallas_call(
        functools.partial(grad_kernel, slab),
        out_shape=jax.ShapeDtypeStruct((y_count, tall, LANES), BF16),
        in_specs=[VMEM] * 3,
        out_specs=VMEM,
        scratch_shapes=[
            pltpu.VMEM((all_rows + 8, LANES), F32),
            pltpu.VMEM((width, LANES), F32),
        ],
        compiler_params=PARAMS,
        name="grads",
    )(parts, act_copy, cot_copy)
    column = lax.all_to_all(slabs, dp[0], 0, 0)
    half = -(-rows // 4) * 4
    line = pl.pallas_call(
        functools.partial(slab_kernel, rows),
        out_shape=jax.ShapeDtypeStruct((z_count, tall + 2 * half, LANES), BF16),
        in_specs=[VMEM] * 3,
        out_specs=VMEM,
        scratch_shapes=[pltpu.VMEM((tall + 2 * half, LANES), F32)],
        compiler_params=PARAMS,
        name="slab",
    )(column, first_moment, second_moment)
    line = lax.all_to_all(line, dp[1], 0, 0)
    own_one, own_two, send = pl.pallas_call(
        functools.partial(owner_kernel, rows, dp[1]),
        out_shape=(
            jax.ShapeDtypeStruct((half, LANES), F32),
            jax.ShapeDtypeStruct((half, LANES), F32),
            jax.ShapeDtypeStruct((y_count, 2 * slab, LANES), BF16),
        ),
        in_specs=[VMEM] * 3,
        out_specs=(VMEM, VMEM, VMEM),
        scratch_shapes=[pltpu.VMEM((tall, LANES), F32)] * 3
        + [pltpu.VMEM((half, LANES), F32)] * 2
        + [pltpu.VMEM((2 * slab, LANES), F32)],
        compiler_params=PARAMS,
        name="owner",
    )(line, first_moment, second_moment)
    moments = lax.all_to_all(send, dp[0], 0, 0)
    partition, written = pl.pallas_call(
        functools.partial(written_kernel, rows, dp),
        out_shape=(
            jax.ShapeDtypeStruct((3, 1, part_len), F32),
            jax.ShapeDtypeStruct((3, all_rows, LANES), F32),
        ),
        in_specs=[VMEM] * 5,
        out_specs=(HBM, HBM),
        scratch_shapes=[
            pltpu.VMEM((all_rows, LANES), F32),
            pltpu.VMEM((all_rows, LANES), F32),
            pltpu.VMEM((3, all_rows, LANES), F32),
            pltpu.VMEM((3, 1, part_len), F32),
            pltpu.SemaphoreType.DMA((5,)),
        ],
        compiler_params=PARAMS,
        name="written",
    )(own_one, own_two, moments, flat_param, mask)
    return (partition, written.reshape(3, 1, 1, all_rows * LANES))


def solution(mesh):
    fine = Mesh(mesh.devices.reshape(8, 12, 4, 2), ("y", "z", "x", "c"))
    return on_mesh(fine)


def on_mesh(fine):
    dp, tensor = ("y", "z"), ("x", "c")
    in_specs = (
        P(dp, tensor),
        P(dp, tensor),
        P(tensor, None),
        P(None, tensor),
        P(tensor, dp),
        P(tensor, dp),
        P(tensor, None),
        P(tensor, None),
    )
    out_specs = (P(None, tensor, dp), P(None, dp, tensor, None))
    return jax.shard_map(
        functools.partial(body, dp), mesh=fine, in_specs=in_specs, out_specs=out_specs, check_vma=False
    )
```

```python
import functools

import jax
import jax.numpy as jnp
from jax import lax
from jax.experimental import pallas as pl
from jax.experimental.pallas import tpu as pltpu
from jax.sharding import Mesh, PartitionSpec as P

BF16 = jnp.bfloat16
F32 = jnp.float32
LANES = 128
VMEM = pl.BlockSpec(memory_space=pltpu.VMEM)
HBM = pl.BlockSpec(memory_space=pltpu.HBM)
NT = (((1,), (1,)), ((), ()))
PARAMS = pltpu.CompilerParams(vmem_limit_bytes=16 * 1024 * 1024)


def store_flat(flat, wide, down_t2, up):
    width = up.shape[1]
    rank = up.shape[0]
    half = width // 2
    per_row = width // LANES
    wide[...] = down_t2.T
    even = wide[pl.ds(0, half, stride=2), :]
    odd = wide[pl.ds(1, half, stride=2), :]
    lane = lax.broadcasted_iota(jnp.int32, (half, LANES), 1)
    flat[0:half, :] = jnp.where(lane < rank, even, odd)
    for c in range(per_row):
        flat[pl.ds(half + c, rank, stride=per_row), :] = up[:, c * LANES : (c + 1) * LANES]
    used = half + rank * per_row
    flat[used:, :] = jnp.zeros((flat.shape[0] - used, LANES), F32)


def mark_pieces(dp, lengths, writers, mask):
    me = lax.axis_index(dp)
    mask[...] = jnp.zeros_like(mask)
    block = 8 * LANES
    spot = lax.broadcasted_iota(jnp.int32, (8, LANES), 0) * LANES + lax.broadcasted_iota(
        jnp.int32, (8, LANES), 1
    )

    def piece(k, start):
        end = start + lengths[0, k]

        @pl.when(writers[0, k] == me)
        def _():
            def mark(b, carry):
                here = spot + b * block
                at = pl.ds(pl.multiple_of(b * 8, 8), 8)
                inside = jnp.logical_and(here >= start, here < end)
                mask[at, :] = jnp.where(inside, 1.0, mask[at, :])
                return carry

            lax.fori_loop(start // block, (end + block - 1) // block, mark, 0)

        return end

    group = 8
    begin = jnp.int32(0)
    for low in range(0, lengths.shape[1], group):
        hit = writers[0, low] == me
        total = lengths[0, low]
        for k in range(low + 1, low + group):
            hit = jnp.logical_or(hit, writers[0, k] == me)
            total += lengths[0, k]

        @pl.when(hit)
        def _(low=low, begin=begin):
            lax.fori_loop(low, low + group, piece, begin)

        begin += total


def low_rank_kernel(
    dp, act, cot, down_t, up, lengths, writers, out, a, c, flat, mask, d, u, wide, long, who, sems
):
    pairs = ((down_t, d), (up, u), (act, a), (cot, c), (lengths, long), (writers, who))
    copies = [pltpu.make_async_copy(source, target, sems.at[i]) for i, (source, target) in enumerate(pairs)]
    for copy in copies:
        copy.start()
    copies[0].wait()
    copies[1].wait()
    left, right = d[...], u[...]
    store_flat(flat, wide, jnp.concatenate([left, left], axis=0), right)
    down_b, up_b = left.astype(BF16), right.astype(BF16)
    blank = jnp.zeros_like(down_b)
    copies[4].wait()
    copies[5].wait()
    mark_pieces(dp, long, who, mask)
    copies[2].wait()
    both = lax.dot_general(a[...], jnp.concatenate([down_b, blank], axis=0), NT, preferred_element_type=F32)
    copies[3].wait()
    both += lax.dot_general(c[...], jnp.concatenate([blank, up_b], axis=0), NT, preferred_element_type=F32)
    out[...] = both.astype(BF16)


def add_copies_kernel(mine, other, out):
    total = mine[...].astype(F32) + other[...].astype(F32)
    tall = out.shape[1]
    for k in range(out.shape[2] // LANES):
        block = total[k * tall : (k + 1) * tall].astype(BF16)
        for i in range(out.shape[0]):
            out[i, :, k * LANES : (k + 1) * LANES] = block


def grad_kernel(rows, parts, act, cot, out, flat, wide):
    wide_total = parts[0].astype(F32)
    for i in range(1, parts.shape[0]):
        wide_total += parts[i].astype(F32)
    total = jnp.concatenate(
        [wide_total[:, k * LANES : (k + 1) * LANES] for k in range(parts.shape[2] // LANES)], axis=0
    )
    turned = total.T.astype(BF16)
    rank = turned.shape[0] // 2
    projected = turned[rank:]
    twice = jnp.concatenate([projected, projected], axis=0)
    up = 2.0 * jnp.dot(turned[:rank], cot[...], preferred_element_type=F32)
    down = 2.0 * jnp.dot(twice, act[...], preferred_element_type=F32)
    store_flat(flat, wide, down, up)
    part = out.shape[1]
    for j in range(out.shape[0]):
        for i in range(out.shape[2] // LANES):
            at = rows * j + part * i
            out[j, :, i * LANES : (i + 1) * LANES] = flat[at : at + part, :].astype(BF16)


def adam_moments(grad, moment_one, moment_two):
    return 0.9 * moment_one + 0.1 * grad, 0.999 * moment_two + 0.001 * grad * grad


def adam_param(param, fresh_one, fresh_two):
    fixed_one = 1.0 - 0.9**10
    fixed_two = 1.0 - 0.999**10
    return param - 0.01 * (fresh_one / fixed_one) / (jnp.sqrt(fresh_two / fixed_two) + 1e-08)


def own_moments(rows, first, second, one, two):
    for r in range(rows):
        one[r : r + 1, :] = first[:, r * LANES : (r + 1) * LANES]
        two[r : r + 1, :] = second[:, r * LANES : (r + 1) * LANES]
    blank = jnp.zeros((one.shape[0] - rows, LANES), F32)
    one[rows:, :] = blank
    two[rows:, :] = blank


def owner_kernel(rows, parts, first, second, fresh_one, fresh_two, send, grad, one, two, both):
    total = jnp.sum(parts[...].astype(F32), axis=0)
    part = total.shape[0]
    for i in range(total.shape[1] // LANES):
        grad[part * i : part * (i + 1), :] = total[:, i * LANES : (i + 1) * LANES]
    own_moments(rows, first, second, one, two)
    fresh = adam_moments(grad[...], one[...], two[...])
    fresh_one[...], fresh_two[...] = fresh
    for i in range(2):
        for r in range(rows):
            both[i : i + 1, r * LANES : (r + 1) * LANES] = fresh[i][r : r + 1, :]
    packed = both[...].astype(BF16)
    for j in range(send.shape[0]):
        send[j] = packed


def row_kernel(source, out, wide):
    count = source.shape[0]
    for z in range(count):
        pair = source[z].astype(F32)
        for i in range(2):
            wide[i * count + z : i * count + z + 1, :] = pair[i : i + 1]
    values = wide[...].astype(BF16)
    for y in range(out.shape[0]):
        out[y] = values


def written_kernel(rows, dp, own_one, own_two, moments, flat, mask, own, out, one, two, fresh, mine, sems):
    count = moments.shape[1] // 2
    steps = sems.shape[0] - 1
    per_step = moments.shape[0] // steps
    tall = per_step * count * rows
    values = own_one[...], own_two[...]
    values = (adam_param(flat[pl.ds(lax.axis_index(dp) * rows, own_one.shape[0]), :], *values),) + values
    for i in range(3):
        for r in range(rows):
            mine[i, :, r * LANES : (r + 1) * LANES] = values[i][r : r + 1, :]
    copies = [pltpu.make_async_copy(mine, own, sems.at[steps])]
    copies[0].start()
    for s in range(steps):
        for y in range(s * per_step, (s + 1) * per_step):
            for r in range(rows):
                values = moments[y, :, r * LANES : (r + 1) * LANES].astype(F32)
                at = pl.ds(y * count * rows + r, count, stride=rows)
                one[at, :] = values[:count]
                two[at, :] = values[count:]
        for r in range(s * tall, (s + 1) * tall, 24):
            at = slice(r, r + 24)
            keep = mask[at, :] > 0.0
            fresh_one, fresh_two = one[at, :], two[at, :]
            updated = adam_param(flat[at, :], fresh_one, fresh_two)
            for i, values in enumerate((updated, fresh_one, fresh_two)):
                fresh[i, at, :] = jnp.where(keep, values, 0.0)
        block = pl.ds(s * tall, tall)
        copies.append(pltpu.make_async_copy(fresh.at[:, block], out.at[:, block], sems.at[s]))
        copies[-1].start()
    for copy in copies:
        copy.wait()


def body(dp, activations, cotangent, factor_down, factor_up, first_moment, second_moment, piece_lengths, writers):
    dp_count = lax.axis_size(dp)
    part_len = first_moment.shape[1]
    rows = part_len // LANES
    all_rows = rows * dp_count
    part = 4
    lanes = -(-rows // part) * LANES
    tokens, width = activations.shape
    rank = factor_up.shape[0]
    down_t = factor_down.T
    x_count = lax.axis_size("x")

    first_in = (activations, cotangent, down_t, factor_up, piece_lengths, writers)
    partial, act_copy, cot_copy, flat_param, mask = pl.pallas_call(
        functools.partial(low_rank_kernel, dp),
        out_shape=(
            jax.ShapeDtypeStruct((tokens, 2 * rank), BF16),
            jax.ShapeDtypeStruct((tokens, width), BF16),
            jax.ShapeDtypeStruct((tokens, width), BF16),
            jax.ShapeDtypeStruct((all_rows + 8, LANES), F32),
            jax.ShapeDtypeStruct((all_rows, LANES), F32),
        ),
        in_specs=[HBM] * 6,
        out_specs=[VMEM] * 5,
        scratch_shapes=[
            pltpu.VMEM((rank, width), F32),
            pltpu.VMEM((rank, width), F32),
            pltpu.VMEM((width, LANES), F32),
            pltpu.SMEM(piece_lengths.shape, jnp.int32),
            pltpu.SMEM(writers.shape, jnp.int32),
            pltpu.SemaphoreType.DMA((6,)),
        ],
        compiler_params=PARAMS,
        name="low_rank",
    )(*[pltpu.with_memory_space_constraint(v, pltpu.HBM) for v in first_in])
    other = lax.ppermute(partial, "c", [(0, 1), (1, 0)])
    copies = pl.pallas_call(
        add_copies_kernel,
        out_shape=jax.ShapeDtypeStruct((x_count, 16, tokens // 16 * 2 * rank), BF16),
        in_specs=[VMEM] * 2,
        out_specs=VMEM,
        compiler_params=PARAMS,
        name="add_cores",
    )(partial, other)
    parts = lax.all_to_all(copies, "x", 0, 0)
    chunks = pl.pallas_call(
        functools.partial(grad_kernel, rows),
        out_shape=jax.ShapeDtypeStruct((dp_count, part, lanes), BF16),
        in_specs=[VMEM] * 3,
        out_specs=VMEM,
        scratch_shapes=[
            pltpu.VMEM((all_rows + 8, LANES), F32),
            pltpu.VMEM((width, LANES), F32),
        ],
        compiler_params=PARAMS,
        name="grads",
    )(parts, act_copy, cot_copy)
    mine = lax.all_to_all(chunks, dp, 0, 0)
    half = lanes * part // LANES
    z_count = lax.axis_size(dp[1])
    own_one, own_two, send = pl.pallas_call(
        functools.partial(owner_kernel, rows),
        out_shape=(
            jax.ShapeDtypeStruct((half, LANES), F32),
            jax.ShapeDtypeStruct((half, LANES), F32),
            jax.ShapeDtypeStruct((z_count, 2, part_len), BF16),
        ),
        in_specs=[VMEM] * 3,
        out_specs=(VMEM, VMEM, VMEM),
        scratch_shapes=[pltpu.VMEM((half, LANES), F32)] * 3 + [pltpu.VMEM((2, part_len), F32)],
        compiler_params=PARAMS,
        name="owner",
    )(mine, first_moment, second_moment)
    row = lax.all_to_all(send, dp[1], 0, 0)
    row_copies = pl.pallas_call(
        row_kernel,
        out_shape=jax.ShapeDtypeStruct((lax.axis_size(dp[0]), 2 * z_count, part_len), BF16),
        in_specs=[VMEM],
        out_specs=VMEM,
        scratch_shapes=[pltpu.VMEM((2 * z_count, part_len), F32)],
        compiler_params=PARAMS,
        name="row_copies",
    )(row)
    moments = lax.all_to_all(row_copies, dp[0], 0, 0)
    partition, written = pl.pallas_call(
        functools.partial(written_kernel, rows, dp),
        out_shape=(
            jax.ShapeDtypeStruct((3, 1, part_len), F32),
            jax.ShapeDtypeStruct((3, all_rows, LANES), F32),
        ),
        in_specs=[VMEM] * 5,
        out_specs=(HBM, HBM),
        scratch_shapes=[
            pltpu.VMEM((all_rows, LANES), F32),
            pltpu.VMEM((all_rows, LANES), F32),
            pltpu.VMEM((3, all_rows, LANES), F32),
            pltpu.VMEM((3, 1, part_len), F32),
            pltpu.SemaphoreType.DMA((5,)),
        ],
        compiler_params=PARAMS,
        name="written",
    )(own_one, own_two, moments, flat_param, mask)
    return (partition, written.reshape(3, 1, 1, all_rows * LANES))


def solution(mesh):
    fine = Mesh(mesh.devices.reshape(8, 12, 4, 2), ("y", "z", "x", "c"))
    return on_mesh(fine)


def on_mesh(fine):
    dp, tensor = ("y", "z"), ("x", "c")
    in_specs = (
        P(dp, tensor),
        P(dp, tensor),
        P(tensor, None),
        P(None, tensor),
        P(tensor, dp),
        P(tensor, dp),
        P(tensor, None),
        P(tensor, None),
    )
    out_specs = (P(None, tensor, dp), P(None, dp, tensor, None))
    return jax.shard_map(
        functools.partial(body, dp), mesh=fine, in_specs=in_specs, out_specs=out_specs, check_vma=False
    )
```
